512 devices in a mesh: seq: 32 (over x, z_hi, y), head: 16 (over z_lo, core).
Axes of the slice: x: 4, y: 4, z: 16 (z_hi: 2, z_lo: 8; z = z_hi * 8 + z_lo), core: 2. Of those that a mesh axis runs over, the one named last changes fastest.
Arguments:
- queries: bfloat16 [4096, 8192], P('seq', 'head'), may hold values from -40 to 40
- long_keys: bfloat16 [4096, 128], P(('seq', 'head')), may hold values from -6 to 6
- long_values: bfloat16 [4096, 128], P(('seq', 'head')), may hold values from -6 to 6
- short_keys: bfloat16 [4096, 128], P(('seq', 'head')), may hold values from -6 to 6
- short_values: bfloat16 [4096, 128], P(('seq', 'head')), may hold values from -6 to 6
- w_out: bfloat16 [8192, 8192], P('head', 'seq'), may hold values from -0.375 to 0.375
Outputs:
- projected: bfloat16 [4096, 8192], P('seq', 'head')
The draws below stay inside these ranges and needn't reach their ends.
All inputs are finite; a program needn't handle non-finite values.
Results may differ from the reference program's by a relative error of at most 0.024.
Values may be sent and summed in bfloat16 or wider, within the bound.
No kernel may reach another device: no remote copies, remote signals or barrier semaphores. Data moves between devices by JAX's collectives and lax.ppermute only.
A program may use at most 64 MiB of HBM per device.

```python
import math
import jax
import jax.numpy as jnp
from jax import lax

D = 8192
DH = 128
W1 = 512
W2 = 32
QB = 32
HEADS = 64
TOKENS = 4096


def shared_keys(key):
    first_keys = jnp.clip(jax.random.normal(jax.random.fold_in(key, 11), (TOKENS, DH), jnp.float32), -6.0, 6.0)
    second_keys = jnp.clip(jax.random.normal(jax.random.fold_in(key, 12), (TOKENS, DH), jnp.float32), -6.0, 6.0)
    return (first_keys, second_keys)


def draw_queries(key, part):
    key = jax.random.fold_in(key, 3)
    base = jax.random.normal(key, (TOKENS, HEADS * DH), jnp.float32)
    return jnp.clip(base, -40.0, 40.0).astype(jnp.bfloat16)


def draw_long_keys(key, part):
    first_keys, second_keys = shared_keys(key)
    return first_keys.astype(jnp.bfloat16)


def draw_short_keys(key, part):
    first_keys, second_keys = shared_keys(key)
    return second_keys.astype(jnp.bfloat16)


def steps_of(key, extent, shards, low, high):
    loudness, own = 1.0, jax.random.fold_in(key, 6)
    for position, shards_of in shards:
        draws = jnp.exp(jax.random.uniform(jax.random.fold_in(own, position), (shards_of,), jnp.float32, low / len(shards), high / len(shards)))
        loudness = loudness * jnp.repeat(draws, extent[position] // shards_of).reshape([-1 if axis == position else 1 for axis in range(len(extent))])
    return loudness


def bell_draw(key, extent, scale, most, cuts=(), held_as=jnp.bfloat16):
    drawn = scale * jax.random.normal(key, extent, jnp.float32)
    if cuts:
        drawn = drawn * steps_of(key, extent, cuts, -0.22, 0.18)
    return jnp.clip(drawn, -most, most).astype(held_as)


def setup_inputs(seed: int = 0) -> dict:
    key_of = jax.random.split(jax.random.key(seed), 7)
    queries = draw_queries(jax.random.fold_in(key_of[6], 71), 0)
    long_keys = draw_long_keys(jax.random.fold_in(key_of[6], 71), 0)
    long_values = bell_draw(key_of[2], (TOKENS, DH), 1.0, 6.0, ((0, 512),))
    short_keys = draw_short_keys(jax.random.fold_in(key_of[6], 71), 0)
    short_values = bell_draw(key_of[4], (TOKENS, DH), 1.0, 6.0, ((0, 512),))
    w_out = bell_draw(key_of[5], (HEADS * DH, D), 256 ** -0.5, 0.375, ((0, 16), (1, 32)))
    return dict(queries=queries, long_keys=long_keys, long_values=long_values, short_keys=short_keys, short_values=short_values, w_out=w_out)


def attend(chosen, first_keys, first_values, second_keys, second_values, first):
    rows = chosen.shape[0]
    span = second_keys.shape[0] - rows + 1
    reach = first_keys.shape[0] - rows
    width = chosen.shape[1]
    key_window = jnp.stack([second_keys[span - 1 - offset:span - 1 - offset + rows] for offset in range(span)], axis=1)
    value_window = jnp.stack([second_values[span - 1 - offset:span - 1 - offset + rows] for offset in range(span)], axis=1)
    mixed = (chosen.astype(jnp.float32)[:, None, :] * key_window.astype(jnp.float32)).astype(jnp.bfloat16)
    scores = jnp.dot(mixed.reshape(rows * span, width).astype(jnp.float32), first_keys.astype(jnp.float32).T, precision=lax.Precision.HIGHEST) * (2.5 / math.sqrt(width))
    scores = scores.reshape(rows, span, reach + rows)
    row_ids = jnp.arange(rows, dtype=jnp.int32)[:, None, None]
    offsets = jnp.arange(span, dtype=jnp.int32)[None, :, None]
    columns = jnp.arange(reach + rows, dtype=jnp.int32)[None, None, :]
    valid = (columns >= row_ids + 1) & (columns <= reach + row_ids) & (first - reach + columns >= 0) & (first + row_ids - offsets >= 0)
    scores = jnp.where(valid, scores, -jnp.inf)
    top = lax.optimization_barrier(jnp.max(scores, axis=(1, 2), keepdims=True))
    weights = jnp.exp(scores - top)
    total = lax.optimization_barrier(jnp.sum(weights, axis=(1, 2)))
    probs = weights.astype(jnp.bfloat16)
    carried = jnp.dot(probs.reshape(rows * span, reach + rows).astype(jnp.float32), first_values.astype(jnp.float32), precision=lax.Precision.HIGHEST).reshape(rows, span, width)
    attended = lax.optimization_barrier(jnp.sum(carried * value_window.astype(jnp.float32), axis=1)) / total[:, None]
    return attended.astype(jnp.bfloat16)

def reference(queries, long_keys, long_values, short_keys, short_values, w_out):
    width = long_keys.shape[1]
    tokens = queries.shape[0]
    heads = queries.shape[1] // width
    first_keys = jnp.concatenate([jnp.zeros((W1, width), jnp.bfloat16), long_keys], axis=0)
    first_values = jnp.concatenate([jnp.zeros((W1, width), jnp.bfloat16), long_values], axis=0)
    second_keys = jnp.concatenate([jnp.zeros((W2 - 1, width), jnp.bfloat16), short_keys], axis=0)
    second_values = jnp.concatenate([jnp.zeros((W2 - 1, width), jnp.bfloat16), short_values], axis=0)
    per_head = queries.reshape(tokens, heads, width).transpose(1, 0, 2)
    batched = jax.vmap(attend, in_axes=(0, None, None, None, None, None))

    def one_block(number):
        start = (number * QB).astype(jnp.int32)
        chosen = lax.dynamic_slice_in_dim(per_head, start, QB, 1)
        keys_one = lax.dynamic_slice_in_dim(first_keys, start, W1 + QB, 0)
        values_one = lax.dynamic_slice_in_dim(first_values, start, W1 + QB, 0)
        keys_two = lax.dynamic_slice_in_dim(second_keys, start, QB + W2 - 1, 0)
        values_two = lax.dynamic_slice_in_dim(second_values, start, QB + W2 - 1, 0)
        return batched(chosen, keys_one, values_one, keys_two, values_two, start)
    results = lax.map(one_block, jnp.arange(tokens // QB, dtype=jnp.int32))
    attended = results.transpose(0, 2, 1, 3).reshape(tokens, heads * width)
    return jnp.dot(attended.astype(jnp.float32), w_out.astype(jnp.float32), precision=lax.Precision.HIGHEST).astype(jnp.bfloat16)
```

```python
import functools
import math

import jax
import jax.numpy as jnp
from jax import lax
from jax.experimental import pallas as pl
from jax.experimental.pallas import tpu as pltpu
from jax.sharding import PartitionSpec as P

W1 = 512
W2 = 32
XS, HS, YS, ZS, CS = 4, 2, 4, 8, 2
BOTH = ("seq", "head")


def seq_of(x, half, y):
    return (x % XS) * HS * YS + (half % HS) * YS + y % YS


def moved(value, target):
    pairs = []
    for x in range(XS):
        for half in range(HS):
            for y in range(YS):
                for z in range(ZS):
                    for c in range(CS):
                        to = target(x, half, y, z, c)
                        if to is None:
                            continue
                        source = seq_of(x, half, y) * ZS * CS + z * CS + c
                        pairs.append((source, seq_of(*to[:3]) * ZS * CS + to[3] * CS + to[4]))
    return lax.ppermute(value, BOTH, pairs)


def later(value, steps):
    count = XS * HS * YS
    return lax.ppermute(value, "seq", [(s, s + steps) for s in range(count - steps)])


def attention_kernel(origin, q_ref, k_ref, v_ref, sk_ref, sv_ref, out_ref, q32, out32, *, tokens):
    rows, wide = q_ref.shape
    width = k_ref.shape[1]
    heads = wide // width
    span = sk_ref.shape[0] - rows
    factor = 2.5 / math.sqrt(width) * math.log2(math.e)
    q32[...] = q_ref[...].astype(jnp.float32)
    lanes = lax.broadcasted_iota(jnp.int32, (tokens, span, width), 2)
    token_of = lax.broadcasted_iota(jnp.int32, (tokens, span, width), 0)
    back = span - 1 - lax.broadcasted_iota(jnp.int32, (tokens, span, width), 1)

    def block(number, carry):
        start = pl.multiple_of(number * tokens, tokens)
        late = (lanes > start + token_of).reshape(tokens * span, width)
        counted = (origin[0] + start + token_of >= back).astype(jnp.float32)
        keys = jnp.stack([sk_ref[pl.ds(start + 1 + i, span), :] for i in range(tokens)])
        values = jnp.stack([sv_ref[pl.ds(start + 1 + i, span), :] for i in range(tokens)])
        for head in range(heads):
            cols = slice(head * width, (head + 1) * width)
            chosen = q32[pl.ds(start, tokens), cols]
            mixed = (chosen[:, None, :] * keys).astype(jnp.bfloat16).reshape(tokens * span, width)
            scores = lax.dot_general(
                mixed, k_ref[...], (((1,), (1,)), ((), ())), preferred_element_type=jnp.float32
            )
            parts = [scores[:, i * width : (i + 1) * width] for i in range(5)]
            parts = [jnp.where(late, parts[0], parts[4])] + parts[1:4]
            top = jnp.maximum(jnp.maximum(parts[0], parts[1]), jnp.maximum(parts[2], parts[3]))
            top = jnp.max(top.reshape(tokens, span, width), axis=1)
            top = jnp.max(top, axis=1, keepdims=True)
            top = jnp.broadcast_to(top[:, :, None], (tokens, span, width))
            top = top.reshape(tokens * span, width)
            weights = [jnp.exp2((p - top) * factor) for p in parts]
            probs = [jnp.where(late, weights[0], 0.0)] + weights[1:]
            probs = probs + [jnp.where(late, 0.0, weights[0])]
            probs = jnp.concatenate([p.astype(jnp.bfloat16) for p in probs], axis=1)
            carried = jnp.dot(probs, v_ref[...], preferred_element_type=jnp.float32)
            above = jnp.sum(carried[:, :width].reshape(tokens, span, width) * values, axis=1)
            below = jnp.sum(carried[:, width:].reshape(tokens, span, width) * counted, axis=1)
            out32[pl.ds(start, tokens), cols] = above / below
        return carry

    lax.fori_loop(0, rows // tokens, block, 0)
    out_ref[...] = out32[...].astype(jnp.bfloat16)


def attention(origin, q, k, v, sk, sv):
    rows, wide = q.shape
    return pl.pallas_call(
        functools.partial(attention_kernel, tokens=16),
        out_shape=jax.ShapeDtypeStruct((rows, wide), jnp.bfloat16),
        in_specs=[pl.BlockSpec(memory_space=pltpu.SMEM)]
        + [pl.BlockSpec(memory_space=pltpu.VMEM)] * 5,
        out_specs=pl.BlockSpec(memory_space=pltpu.VMEM),
        scratch_shapes=[pltpu.VMEM((rows, wide), jnp.float32)] * 2,
        compiler_params=pltpu.CompilerParams(vmem_limit_bytes=40 * 2**20),
        cost_estimate=pl.CostEstimate(
            flops=20_000_000_000, bytes_accessed=2**20, transcendentals=0
        ),
    )(origin, q, k, v, sk, sv)


def in_order(first, second, swap):
    return jnp.where(swap, second, first), jnp.where(swap, first, second)


def per_device(queries, long_keys, long_values, short_keys, short_values, w_out):
    rows = queries.shape[0]
    width = long_keys.shape[1]
    seq = lax.axis_index("seq")
    head = lax.axis_index("head")
    x, half, y = seq // (HS * YS), seq // YS % HS, seq % YS
    c = head % CS
    origin = seq * rows

    piece = jnp.stack([long_keys, long_values, short_keys, short_values])
    before = later(piece, 1)
    older = [later(piece[:2], steps) for steps in range(2, W1 // rows + 1)]
    blocks = older[::-1] + [before[:2], piece[:2]]
    mine = jnp.concatenate(
        [jnp.stack([b[0] for b in blocks]), jnp.stack([b[1] for b in blocks]), before[2:], piece[2:]]
    )
    gathered = lax.all_gather(mine, "head", axis=1, tiled=True)
    spots = len(blocks)
    reach = (spots - 1) * rows
    keys = gathered[:spots].reshape(spots * rows, width)
    values = gathered[spots : 2 * spots].reshape(spots * rows, width)
    place = origin - reach + jnp.arange(spots * rows, dtype=jnp.int32)[:, None]
    first_key = lax.dynamic_slice_in_dim(keys, jnp.maximum(reach - origin, 0), 1, 0)
    keys = jnp.where(place >= 0, keys, first_key)
    ones = (place >= 0).astype(jnp.bfloat16) * jnp.ones((1, width), jnp.bfloat16)
    values = jnp.concatenate([values, ones], axis=1)
    near = gathered[2 * spots :].astype(jnp.float32)
    near_keys = jnp.concatenate([near[0, rows - W2 :], near[2]])
    near_values = jnp.concatenate([near[1, rows - W2 :], near[3]])
    near_place = origin - W2 + jnp.arange(W2 + rows, dtype=jnp.int32)[:, None]
    near_keys = jnp.where(near_place >= 0, near_keys, near_keys[W2 : W2 + 1])

    other = moved(w_out, lambda x, h, y, z, c: (x, h + 1, y, z, c))
    pair = jnp.stack(in_order(w_out, other, half == 1))
    pair, keys = lax.optimization_barrier((pair, keys))
    from_x = [pair] + [
        moved(pair, lambda x, h, y, z, c, d=d: (x - d, h, y, z, c)) for d in (1, 2, 3)
    ]
    attended = attention(
        origin.reshape(1), queries, keys, values, near_keys, near_values
    )

    attended, from_x = lax.optimization_barrier((attended, from_x))

    from_y = [attended] + [
        moved(attended, lambda x, h, y, z, c, d=d: (x, h, y - d, z, c)) for d in (1, 2, 3)
    ]
    twice = jnp.concatenate(from_y + from_y[:3])
    tokens = lax.dynamic_slice_in_dim(twice, (2 * c - y) % YS * rows, YS * rows, 0)
    twice = jnp.concatenate(from_x + from_x[:3])
    columns = lax.dynamic_slice_in_dim(twice, (XS - x) % XS * HS, XS * HS, 0)
    count = YS // 2 * rows
    product = functools.partial(
        jnp.einsum, "tk,nkc->ntc", preferred_element_type=jnp.float32
    )
    away = product(tokens[count:], columns).astype(jnp.bfloat16)
    came = moved(away, lambda x, h, y, z, c: (x, h, y, z, 1 - c))
    kept = (product(tokens[:count], columns) + came.astype(jnp.float32)).astype(jnp.bfloat16)
    groups = [[z * CS + core for z in range(ZS)] for core in range(CS)]
    parts = lax.all_to_all(kept, "head", 0, 0, axis_index_groups=groups, tiled=True)
    summed = jnp.sum(parts.astype(jnp.float32), axis=0).astype(jnp.bfloat16)
    summed = summed.reshape(YS // 2, rows, summed.shape[-1])
    odd = y % 2 == 1
    sent = in_order(summed[0], summed[1], odd)
    landed = [
        moved(
            sent[j],
            lambda x, h, y, z, c, j=j: (x, h, 2 * c + (j ^ (y % 2)), z, y // 2),
        )
        for j in range(2)
    ]
    return jnp.concatenate(in_order(landed[0], landed[1], odd), axis=1)


def solution(mesh):
    return jax.shard_map(
        per_device,
        mesh=mesh,
        in_specs=(
            P("seq", "head"),
            P(("seq", "head"), None),
            P(("seq", "head"), None),
            P(("seq", "head"), None),
            P(("seq", "head"), None),
            P("head", "seq"),
        ),
        out_specs=P("seq", "head"),
        check_vma=False,
    )
```

```python
import functools
import math

import jax
import jax.numpy as jnp
from jax import lax
from jax.experimental import pallas as pl
from jax.experimental.pallas import tpu as pltpu
from jax.sharding import PartitionSpec as P

W1 = 512
W2 = 32
XS, HS, YS, ZS, CS = 4, 2, 4, 8, 2
BOTH = ("seq", "head")


def seq_of(x, half, y):
    return (x % XS) * HS * YS + (half % HS) * YS + y % YS


def moved(value, target):
    pairs = []
    for x in range(XS):
        for half in range(HS):
            for y in range(YS):
                for z in range(ZS):
                    for c in range(CS):
                        to = target(x, half, y, z, c)
                        if to is None:
                            continue
                        source = seq_of(x, half, y) * ZS * CS + z * CS + c
                        pairs.append((source, seq_of(*to[:3]) * ZS * CS + to[3] * CS + to[4]))
    return lax.ppermute(value, BOTH, pairs)


def later(value, steps):
    count = XS * HS * YS
    return lax.ppermute(value, "seq", [(s, s + steps) for s in range(count - steps)])


def attention_kernel(
    place, q_ref, mine_ref, other_ref, out_ref, k_ref, v_ref, sk_ref, sv_ref, q32, out32, *, tokens
):
    rows, wide = q_ref.shape
    width = k_ref.shape[1]
    heads = wide // width
    block_now, core = place[0], place[1]
    spots = W1 // rows + 1

    def whole(number):
        mine = mine_ref[:, number].astype(jnp.float32)
        other = other_ref[:, number].astype(jnp.float32)
        first, second = jnp.where(core == 1, other, mine), jnp.where(core == 1, mine, other)
        return jnp.concatenate([first[:, None], second[:, None]], axis=1).reshape(rows, width)

    for spot in reversed(range(spots)):
        there = block_now + spot >= spots - 1
        span = pl.ds(spot * rows, rows)
        k_ref[span, :] = whole(spot).astype(jnp.bfloat16)
        v_ref[span, :width] = whole(spots + spot).astype(jnp.bfloat16)
        v_ref[span, width:] = jnp.full((rows, width), jnp.where(there, 1.0, 0.0)).astype(jnp.bfloat16)
    for spot in range(1, spots):

        @pl.when(block_now == spots - 1 - spot)
        def _():
            key = whole(spot)[:1]
            filler = jnp.broadcast_to(key, (spot * rows, width))
            k_ref[: spot * rows, :] = filler.astype(jnp.bfloat16)

    short = whole(2 * spots + 2)
    sk_ref[W2:, :] = short
    edge = whole(2 * spots)[rows - W2 :]
    sk_ref[:W2, :] = jnp.where(block_now == 0, jnp.broadcast_to(short[:1], edge.shape), edge)
    sv_ref[W2:, :] = whole(2 * spots + 3)
    sv_ref[:W2, :] = whole(2 * spots + 1)[rows - W2 :]
    origin = block_now * rows

    span = sk_ref.shape[0] - rows
    factor = 2.5 / math.sqrt(width) * math.log2(math.e)
    q32[...] = q_ref[...].astype(jnp.float32)
    lanes = lax.broadcasted_iota(jnp.int32, (tokens, span, width), 2)
    token_of = lax.broadcasted_iota(jnp.int32, (tokens, span, width), 0)
    back = span - 1 - lax.broadcasted_iota(jnp.int32, (tokens, span, width), 1)

    def block(number, carry):
        start = pl.multiple_of(number * tokens, tokens)
        late = (lanes > start + token_of).reshape(tokens * span, width)
        counted = (origin + start + token_of >= back).astype(jnp.float32)
        keys = jnp.stack([sk_ref[pl.ds(start + 1 + i, span), :] for i in range(tokens)])
        values = jnp.stack([sv_ref[pl.ds(start + 1 + i, span), :] for i in range(tokens)])
        for head in range(heads):
            cols = slice(head * width, (head + 1) * width)
            chosen = q32[pl.ds(start, tokens), cols]
            mixed = (chosen[:, None, :] * keys).astype(jnp.bfloat16).reshape(tokens * span, width)
            scores = lax.dot_general(
                mixed, k_ref[...], (((1,), (1,)), ((), ())), preferred_element_type=jnp.float32
            )
            parts = [scores[:, i * width : (i + 1) * width] for i in range(5)]
            parts = [jnp.where(late, parts[0], parts[4])] + parts[1:4]
            top = jnp.maximum(jnp.maximum(parts[0], parts[1]), jnp.maximum(parts[2], parts[3]))
            top = jnp.max(top.reshape(tokens, span, width), axis=1)
            top = jnp.max(top, axis=1, keepdims=True)
            top = jnp.broadcast_to(top[:, :, None], (tokens, span, width))
            top = top.reshape(tokens * span, width)
            weights = [jnp.exp2((p - top) * factor) for p in parts]
            probs = [jnp.where(late, weights[0], 0.0)] + weights[1:]
            probs = probs + [jnp.where(late, 0.0, weights[0])]
            probs = jnp.concatenate([p.astype(jnp.bfloat16) for p in probs], axis=1)
            carried = jnp.dot(probs, v_ref[...], preferred_element_type=jnp.float32)
            above = jnp.sum(carried[:, :width].reshape(tokens, span, width) * values, axis=1)
            below = jnp.sum(carried[:, width:].reshape(tokens, span, width) * counted, axis=1)
            out32[pl.ds(start, tokens), cols] = above / below
        return carry

    lax.fori_loop(0, rows // tokens, block, 0)
    out_ref[...] = out32[...].astype(jnp.bfloat16)


def attention(place, q, mine, other):
    rows, wide = q.shape
    width = mine.shape[-1]
    spots = W1 // rows + 1
    return pl.pallas_call(
        functools.partial(attention_kernel, tokens=16),
        out_shape=jax.ShapeDtypeStruct((rows, wide), jnp.bfloat16),
        in_specs=[pl.BlockSpec(memory_space=pltpu.SMEM)]
        + [pl.BlockSpec(memory_space=pltpu.VMEM)] * 3,
        out_specs=pl.BlockSpec(memory_space=pltpu.VMEM),
        scratch_shapes=[
            pltpu.VMEM((spots * rows, width), jnp.bfloat16),
            pltpu.VMEM((spots * rows, 2 * width), jnp.bfloat16),
            pltpu.VMEM((W2 + rows, width), jnp.float32),
            pltpu.VMEM((W2 + rows, width), jnp.float32),
            pltpu.VMEM((rows, wide), jnp.float32),
            pltpu.VMEM((rows, wide), jnp.float32),
        ],
        compiler_params=pltpu.CompilerParams(vmem_limit_bytes=40 * 2**20),
        cost_estimate=pl.CostEstimate(
            flops=20_000_000_000, bytes_accessed=2**20, transcendentals=0
        ),
    )(place, q, mine, other)


def pack_kernel(count, *refs):
    own, before, older, out_ref = refs[:4], refs[4], refs[5:-1], refs[-1]
    for to in range(out_ref.shape[0]):
        for kind in range(2):
            line = [ref.at[kind] for ref in older[::-1]] + [before.at[kind], own[kind]]
            for spot, ref in enumerate(line):
                out_ref[to, kind * count + spot] = ref[...]
            out_ref[to, 2 * count + kind] = before[2 + kind]
            out_ref[to, 2 * count + 2 + kind] = own[2 + kind][...]


def pack(own, before, older):
    count = len(older) + 2
    return pl.pallas_call(
        functools.partial(pack_kernel, count),
        out_shape=jax.ShapeDtypeStruct((ZS, 2 * count + 4) + own[0].shape, own[0].dtype),
        in_specs=[pl.BlockSpec(memory_space=pltpu.VMEM)] * (5 + len(older)),
        out_specs=pl.BlockSpec(memory_space=pltpu.VMEM),
    )(*own, before, *older)


def project_kernel(place, *refs):
    tokens, columns, out_ref = refs[:YS], refs[YS : YS + XS], refs[-1]
    x, y, c = place[0], place[1], place[2]
    for d in range(XS):
        to = lax.rem(x + d, XS)
        for e in range(YS):
            slot = lax.rem(y + e + YS - 2 * c, YS)
            total = jnp.dot(tokens[e][0], columns[d][0], preferred_element_type=jnp.float32)
            total += jnp.dot(tokens[e][1], columns[d][1], preferred_element_type=jnp.float32)
            out_ref[slot // 2, to, slot % 2] = total.astype(jnp.bfloat16)


def project(place, tokens, columns):
    rows, wide = tokens[0].shape[1], columns[0].shape[2]
    return pl.pallas_call(
        project_kernel,
        out_shape=jax.ShapeDtypeStruct((2, XS, YS // 2, rows, wide), jnp.bfloat16),
        in_specs=[pl.BlockSpec(memory_space=pltpu.SMEM)]
        + [pl.BlockSpec(memory_space=pltpu.VMEM)] * (XS + YS),
        out_specs=pl.BlockSpec(memory_space=pltpu.VMEM),
        compiler_params=pltpu.CompilerParams(vmem_limit_bytes=40 * 2**20),
        cost_estimate=pl.CostEstimate(
            flops=1_100_000_000, bytes_accessed=4 * 2**20, transcendentals=0
        ),
    )(place, *tokens, *columns)


def in_order(first, second, swap):
    return jnp.where(swap, second, first), jnp.where(swap, first, second)


def per_device(queries, long_keys, long_values, short_keys, short_values, w_out):
    rows = queries.shape[0]
    seq = lax.axis_index("seq")
    head = lax.axis_index("head")
    x, half, y = seq // (HS * YS), seq // YS % HS, seq % YS
    z, c = head // CS, head % CS

    def first_hop(x, h, y, z, c):
        return (x, h, y, z ^ 1, c) if h != z % 2 else (x, h + 1, y, z, c)

    def second_hop(x, h, y, z, c):
        return (x, h + 1, y, z ^ 1, c) if h != z % 2 else None

    one_way = moved(w_out, first_hop)
    other_way = moved(w_out, second_hop)

    piece = jnp.stack([long_keys, long_values, short_keys, short_values])
    before = later(piece, 1)
    older = [later(piece[:2], steps) for steps in range(2, W1 // rows + 1)]
    mine = pack((long_keys, long_values, short_keys, short_values), before, older)
    lines = [[z * CS + core for z in range(ZS)] for core in range(CS)]
    over_z = lax.all_to_all(mine, "head", 0, 0, axis_index_groups=lines, tiled=True)
    over_core = moved(over_z, lambda x, h, y, z, c: (x, h, y, z, 1 - c))

    near_by = half == z % 2
    pair = jnp.stack(
        [jnp.where(near_by, w_out, one_way), jnp.where(near_by, one_way, other_way)]
    )
    pair, over_core = lax.optimization_barrier((pair, over_core))
    from_x = [pair] + [
        moved(pair, lambda x, h, y, z, c, d=d: (x - d, h, y, z, c)) for d in (1, 2, 3)
    ]

    attended = attention(jnp.stack([seq, c]), queries, over_z, over_core)
    attended, from_x = lax.optimization_barrier((attended, from_x))

    beside = moved(attended, lambda x, h, y, z, c: (x, h, y, z ^ 1, c))
    attended = jnp.stack([attended, beside])
    from_y = [attended] + [
        moved(attended, lambda x, h, y, z, c, d=d: (x, h, y - d, z, c)) for d in (1, 2, 3)
    ]
    sums = project(jnp.stack([x, y, c]), from_y, from_x)
    came = moved(sums[1], lambda x, h, y, z, c: (x, h, y, z, 1 - c))
    kept = (sums[0].astype(jnp.float32) + came.astype(jnp.float32)).astype(jnp.bfloat16)
    groups = [
        [(2 * far + low) * CS + core for far in range(ZS // 2)]
        for low in range(2)
        for core in range(CS)
    ]
    parts = lax.all_to_all(kept, "head", 0, 0, axis_index_groups=groups, tiled=True)
    summed = jnp.sum(parts.astype(jnp.float32), axis=0).astype(jnp.bfloat16)
    odd = y % 2 == 1
    sent = in_order(summed[0], summed[1], odd)
    landed = [
        moved(
            sent[j],
            lambda x, h, y, z, c, j=j: (x, h, 2 * c + (j ^ (y % 2)), z, y // 2),
        )
        for j in range(2)
    ]
    return jnp.concatenate(in_order(landed[0], landed[1], odd), axis=1)


def solution(mesh):
    return jax.shard_map(
        per_device,
        mesh=mesh,
        in_specs=(
            P("seq", "head"),
            P(("seq", "head"), None),
            P(("seq", "head"), None),
            P(("seq", "head"), None),
            P(("seq", "head"), None),
            P("head", "seq"),
        ),
        out_specs=P("seq", "head"),
        check_vma=False,
    )
```

```python
import functools
import math

import jax
import jax.numpy as jnp
from jax import lax
from jax.experimental import pallas as pl
from jax.experimental.pallas import tpu as pltpu
from jax.sharding import PartitionSpec as P

W1 = 512
W2 = 32
XS, HS, YS, ZS, CS = 4, 2, 4, 8, 2
BOTH = ("seq", "head")


def seq_of(x, half, y):
    return (x % XS) * HS * YS + (half % HS) * YS + y % YS


def moved(value, target):
    pairs = []
    for x in range(XS):
        for half in range(HS):
            for y in range(YS):
                for z in range(ZS):
                    for c in range(CS):
                        to = target(x, half, y, z, c)
                        if to is None:
                            continue
                        source = seq_of(x, half, y) * ZS * CS + z * CS + c
                        pairs.append((source, seq_of(*to[:3]) * ZS * CS + to[3] * CS + to[4]))
    return lax.ppermute(value, BOTH, pairs)


def later(value, steps):
    count = XS * HS * YS
    return lax.ppermute(value, "seq", [(s, s + steps) for s in range(count - steps)])


def attention_kernel(
    place, q_ref, mine_ref, other_ref, out_ref, k_ref, v_ref, sk_ref, sv_ref, q32, out32, *, tokens
):
    rows, wide = q_ref.shape
    width = k_ref.shape[1]
    heads = wide // width
    block_now, core = place[0], place[1]
    spots = W1 // rows + 1

    def whole(number):
        mine = mine_ref[:, number].astype(jnp.float32)
        other = other_ref[:, number].astype(jnp.float32)
        first, second = jnp.where(core == 1, other, mine), jnp.where(core == 1, mine, other)
        return jnp.concatenate([first[:, None], second[:, None]], axis=1).reshape(rows, width)

    for spot in reversed(range(spots)):
        there = block_now + spot >= spots - 1
        span = pl.ds(spot * rows, rows)
        k_ref[span, :] = whole(spot).astype(jnp.bfloat16)
        v_ref[span, :width] = whole(spots + spot).astype(jnp.bfloat16)
        v_ref[span, width:] = jnp.full((rows, width), jnp.where(there, 1.0, 0.0)).astype(jnp.bfloat16)
    for spot in range(1, spots):

        @pl.when(block_now == spots - 1 - spot)
        def _():
            key = whole(spot)[:1]
            filler = jnp.broadcast_to(key, (spot * rows, width))
            k_ref[: spot * rows, :] = filler.astype(jnp.bfloat16)

    short = whole(2 * spots + 2)
    sk_ref[W2:, :] = short
    edge = whole(2 * spots)[rows - W2 :]
    sk_ref[:W2, :] = jnp.where(block_now == 0, jnp.broadcast_to(short[:1], edge.shape), edge)
    sv_ref[W2:, :] = whole(2 * spots + 3)
    sv_ref[:W2, :] = whole(2 * spots + 1)[rows - W2 :]
    origin = block_now * rows

    span = sk_ref.shape[0] - rows
    factor = 2.5 / math.sqrt(width) * math.log2(math.e)
    q32[...] = q_ref[...].astype(jnp.float32)
    lanes = lax.broadcasted_iota(jnp.int32, (tokens, span, width), 2)
    token_of = lax.broadcasted_iota(jnp.int32, (tokens, span, width), 0)
    back = span - 1 - lax.broadcasted_iota(jnp.int32, (tokens, span, width), 1)

    def block(number, carry):
        start = pl.multiple_of(number * tokens, tokens)
        late = (lanes > start + token_of).reshape(tokens * span, width)
        counted = (origin + start + token_of >= back).astype(jnp.float32)
        keys = jnp.stack([sk_ref[pl.ds(start + 1 + i, span), :] for i in range(tokens)])
        values = jnp.stack([sv_ref[pl.ds(start + 1 + i, span), :] for i in range(tokens)])
        for head in range(heads):
            cols = slice(head * width, (head + 1) * width)
            chosen = q32[pl.ds(start, tokens), cols]
            mixed = (chosen[:, None, :] * keys).astype(jnp.bfloat16).reshape(tokens * span, width)
            scores = lax.dot_general(
                mixed, k_ref[...], (((1,), (1,)), ((), ())), preferred_element_type=jnp.float32
            )
            parts = [scores[:, i * width : (i + 1) * width] for i in range(5)]
            parts = [jnp.where(late, parts[0], parts[4])] + parts[1:4]
            top = jnp.maximum(jnp.maximum(parts[0], parts[1]), jnp.maximum(parts[2], parts[3]))
            top = jnp.max(top.reshape(tokens, span, width), axis=1)
            top = jnp.max(top, axis=1, keepdims=True)
            top = jnp.broadcast_to(top[:, :, None], (tokens, span, width))
            top = top.reshape(tokens * span, width)
            weights = [jnp.exp2((p - top) * factor) for p in parts]
            probs = [jnp.where(late, weights[0], 0.0)] + weights[1:]
            probs = probs + [jnp.where(late, 0.0, weights[0])]
            probs = jnp.concatenate([p.astype(jnp.bfloat16) for p in probs], axis=1)
            carried = jnp.dot(probs, v_ref[...], preferred_element_type=jnp.float32)
            above = jnp.sum(carried[:, :width].reshape(tokens, span, width) * values, axis=1)
            below = jnp.sum(carried[:, width:].reshape(tokens, span, width) * counted, axis=1)
            out32[pl.ds(start, tokens), cols] = above / below
        return carry

    lax.fori_loop(0, rows // tokens, block, 0)
    out_ref[...] = out32[...].astype(jnp.bfloat16)


def attention(place, q, mine, other):
    rows, wide = q.shape
    width = mine.shape[-1]
    spots = W1 // rows + 1
    return pl.pallas_call(
        functools.partial(attention_kernel, tokens=16),
        out_shape=jax.ShapeDtypeStruct((rows, wide), jnp.bfloat16),
        in_specs=[pl.BlockSpec(memory_space=pltpu.SMEM)]
        + [pl.BlockSpec(memory_space=pltpu.VMEM)] * 3,
        out_specs=pl.BlockSpec(memory_space=pltpu.VMEM),
        scratch_shapes=[
            pltpu.VMEM((spots * rows, width), jnp.bfloat16),
            pltpu.VMEM((spots * rows, 2 * width), jnp.bfloat16),
            pltpu.VMEM((W2 + rows, width), jnp.float32),
            pltpu.VMEM((W2 + rows, width), jnp.float32),
            pltpu.VMEM((rows, wide), jnp.float32),
            pltpu.VMEM((rows, wide), jnp.float32),
        ],
        compiler_params=pltpu.CompilerParams(vmem_limit_bytes=40 * 2**20),
        cost_estimate=pl.CostEstimate(
            flops=20_000_000_000, bytes_accessed=2**20, transcendentals=0
        ),
    )(place, q, mine, other)


def pack_kernel(count, *refs):
    own, before, older, out_ref = refs[:4], refs[4], refs[5:-1], refs[-1]
    for to in range(out_ref.shape[0]):
        for kind in range(2):
            line = [ref.at[kind] for ref in older[::-1]] + [before.at[kind], own[kind]]
            for spot, ref in enumerate(line):
                out_ref[to, kind * count + spot] = ref[...]
            out_ref[to, 2 * count + kind] = before[2 + kind]
            out_ref[to, 2 * count + 2 + kind] = own[2 + kind][...]


def pack(own, before, older):
    count = len(older) + 2
    return pl.pallas_call(
        functools.partial(pack_kernel, count),
        out_shape=jax.ShapeDtypeStruct((ZS, 2 * count + 4) + own[0].shape, own[0].dtype),
        in_specs=[pl.BlockSpec(memory_space=pltpu.VMEM)] * (5 + len(older)),
        out_specs=pl.BlockSpec(memory_space=pltpu.VMEM),
    )(*own, before, *older)


def project_kernel(place, *refs):
    tokens, columns, out_ref = refs[:YS], refs[YS : YS + XS], refs[-1]
    x, y, c = place[0], place[1], place[2]
    for d in range(XS):
        to = lax.rem(x + d, XS)
        for e in range(YS):
            slot = lax.rem(y + e + YS - 2 * c, YS)
            total = jnp.dot(tokens[e][0], columns[d][0], preferred_element_type=jnp.float32)
            total += jnp.dot(tokens[e][1], columns[d][1], preferred_element_type=jnp.float32)
            out_ref[slot // 2, to, slot % 2] = total.astype(jnp.bfloat16)


def project(place, tokens, columns):
    rows, wide = tokens[0].shape[1], columns[0].shape[2]
    return pl.pallas_call(
        project_kernel,
        out_shape=jax.ShapeDtypeStruct((2, XS, YS // 2, rows, wide), jnp.bfloat16),
        in_specs=[pl.BlockSpec(memory_space=pltpu.SMEM)]
        + [pl.BlockSpec(memory_space=pltpu.VMEM)] * (XS + YS),
        out_specs=pl.BlockSpec(memory_space=pltpu.VMEM),
        compiler_params=pltpu.CompilerParams(vmem_limit_bytes=40 * 2**20),
        cost_estimate=pl.CostEstimate(
            flops=1_100_000_000, bytes_accessed=4 * 2**20, transcendentals=0
        ),
    )(place, *tokens, *columns)


def in_order(first, second, swap):
    return jnp.where(swap, second, first), jnp.where(swap, first, second)


def per_device(queries, long_keys, long_values, short_keys, short_values, w_out):
    rows = queries.shape[0]
    seq = lax.axis_index("seq")
    head = lax.axis_index("head")
    x, half, y = seq // (HS * YS), seq // YS % HS, seq % YS
    z, c = head // CS, head % CS

    def along(steps):
        def target(x, h, y, z, c):
            to = (h * ZS + z + steps) % (HS * ZS)
            return (x, to // ZS, y, to % ZS, c)

        return target

    def kept_here(h, z):
        return h == z % 2

    def first_up(x, h, y, z, c):
        return along(4)(x, h, y, z, c) if kept_here(h, z) else None

    def first_down(x, h, y, z, c):
        return None if kept_here(h, z) else along(-4)(x, h, y, z, c)

    def second_up(x, h, y, z, c):
        spot = (h * ZS + z - 4) % (HS * ZS)
        return along(4)(x, h, y, z, c) if kept_here(spot // ZS, spot % ZS) else None

    def second_down(x, h, y, z, c):
        spot = (h * ZS + z + 4) % (HS * ZS)
        if kept_here(spot // ZS, spot % ZS):
            return None
        return along(-5 if spot < ZS else -3)(x, h, y, z, c)

    def near(x, h, y, z, c):
        return None if kept_here(h, z) else (x, h, y, z ^ 1, c)

    upward, downward = moved(w_out, first_up), moved(w_out, first_down)

    piece = jnp.stack([long_keys, long_values, short_keys, short_values])
    before = later(piece, 1)
    older = [later(piece[:2], steps) for steps in range(2, W1 // rows + 1)]
    mine = pack((long_keys, long_values, short_keys, short_values), before, older)
    lines = [[z * CS + core for z in range(ZS)] for core in range(CS)]
    mine, upward, downward = lax.optimization_barrier((mine, upward, downward))
    upward, downward = moved(upward, second_up), moved(downward, second_down)
    beside = moved(w_out, near)
    over_z = lax.all_to_all(mine, "head", 0, 0, axis_index_groups=lines, tiled=True)
    over_core = moved(over_z, lambda x, h, y, z, c: (x, h, y, z, 1 - c))

    near_by = half == z % 2
    pair = jnp.stack(
        [jnp.where(near_by, w_out, upward), jnp.where(near_by, beside, downward)]
    )
    pair, over_core = lax.optimization_barrier((pair, over_core))
    from_x = [pair] + [
        moved(pair, lambda x, h, y, z, c, d=d: (x - d, h, y, z, c)) for d in (1, 2, 3)
    ]

    attended = attention(jnp.stack([seq, c]), queries, over_z, over_core)
    attended, from_x = lax.optimization_barrier((attended, from_x))

    beside = moved(attended, lambda x, h, y, z, c: (x, h, y, z ^ 1, c))
    attended = jnp.stack([attended, beside])
    from_y = [attended] + [
        moved(attended, lambda x, h, y, z, c, d=d: (x, h, y - d, z, c)) for d in (1, 2, 3)
    ]
    sums = project(jnp.stack([x, y, c]), from_y, from_x)
    came = moved(sums[1], lambda x, h, y, z, c: (x, h, y, z, 1 - c))
    kept = (sums[0].astype(jnp.float32) + came.astype(jnp.float32)).astype(jnp.bfloat16)
    groups = [
        [(2 * far + low) * CS + core for far in range(ZS // 2)]
        for low in range(2)
        for core in range(CS)
    ]
    parts = lax.all_to_all(kept, "head", 0, 0, axis_index_groups=groups, tiled=True)
    summed = jnp.sum(parts.astype(jnp.float32), axis=0).astype(jnp.bfloat16)
    odd = y % 2 == 1
    sent = in_order(summed[0], summed[1], odd)
    landed = [
        moved(
            sent[j],
            lambda x, h, y, z, c, j=j: (x, h, 2 * c + (j ^ (y % 2)), z, y // 2),
        )
        for j in range(2)
    ]
    return jnp.concatenate(in_order(landed[0], landed[1], odd), axis=1)


def solution(mesh):
    return jax.shard_map(
        per_device,
        mesh=mesh,
        in_specs=(
            P("seq", "head"),
            P(("seq", "head"), None),
            P(("seq", "head"), None),
            P(("seq", "head"), None),
            P(("seq", "head"), None),
            P("head", "seq"),
        ),
        out_specs=P("seq", "head"),
        check_vma=False,
    )
```

```python
import functools
import math

import jax
import jax.numpy as jnp
from jax import lax
from jax.experimental import pallas as pl
from jax.experimental.pallas import tpu as pltpu
from jax.sharding import PartitionSpec as P

W1 = 512
W2 = 32
XS, HS, YS, ZS, CS = 4, 2, 4, 8, 2
BOTH = ("seq", "head")


def seq_of(x, half, y):
    return (x % XS) * HS * YS + (half % HS) * YS + y % YS


def moved(value, target):
    pairs = []
    for x in range(XS):
        for half in range(HS):
            for y in range(YS):
                for z in range(ZS):
                    for c in range(CS):
                        to = target(x, half, y, z, c)
                        if to is None:
                            continue
                        source = seq_of(x, half, y) * ZS * CS + z * CS + c
                        pairs.append((source, seq_of(*to[:3]) * ZS * CS + to[3] * CS + to[4]))
    return lax.ppermute(value, BOTH, pairs)


def later(value, steps):
    count = XS * HS * YS
    return lax.ppermute(value, "seq", [(s, s + steps) for s in range(count - steps)])


def window_kernel(
    place, q_ref, mine_ref, other_ref, out_ref, k_ref, v_ref, sk_ref, sv_ref, q32, out32, *, tokens
):
    rows = q_ref.shape[0]
    width = k_ref.shape[1]
    block_now, core = place[0], place[1]
    spots = W1 // rows + 1

    def whole(number):
        mine = mine_ref[:, number].astype(jnp.float32)
        other = other_ref[:, number].astype(jnp.float32)
        first, second = jnp.where(core == 1, other, mine), jnp.where(core == 1, mine, other)
        return jnp.concatenate([first[:, None], second[:, None]], axis=1).reshape(rows, width)

    for spot in reversed(range(spots)):
        there = block_now + spot >= spots - 1
        span = pl.ds(spot * rows, rows)
        k_ref[span, :] = whole(spot).astype(jnp.bfloat16)
        v_ref[span, :width] = whole(spots + spot).astype(jnp.bfloat16)
        v_ref[span, width:] = jnp.full((rows, width), jnp.where(there, 1.0, 0.0)).astype(jnp.bfloat16)
    for spot in range(1, spots):

        @pl.when(block_now == spots - 1 - spot)
        def _():
            key = whole(spot)[:1]
            filler = jnp.broadcast_to(key, (spot * rows, width))
            k_ref[: spot * rows, :] = filler.astype(jnp.bfloat16)

    short = whole(2 * spots + 2)
    sk_ref[W2:, :] = short
    edge = whole(2 * spots)[rows - W2 :]
    sk_ref[:W2, :] = jnp.where(block_now == 0, jnp.broadcast_to(short[:1], edge.shape), edge)
    sv_ref[W2:, :] = whole(2 * spots + 3)
    sv_ref[:W2, :] = whole(2 * spots + 1)[rows - W2 :]
    attend_half(place, q_ref, k_ref, v_ref, sk_ref, sv_ref, q32, out32, tokens, 0)
    out_ref[...] = out32[: rows // 2].astype(jnp.bfloat16)


def attend_half(place, q_ref, k_ref, v_ref, sk_ref, sv_ref, q32, out32, tokens, part):
    rows, wide = q_ref.shape
    width = k_ref.shape[1]
    heads = wide // width
    origin = place[0] * rows
    span = sk_ref.shape[0] - rows
    factor = 2.5 / math.sqrt(width) * math.log2(math.e)
    q32[...] = q_ref[...].astype(jnp.float32)
    lanes = lax.broadcasted_iota(jnp.int32, (tokens, span, width), 2)
    token_of = lax.broadcasted_iota(jnp.int32, (tokens, span, width), 0)
    back = span - 1 - lax.broadcasted_iota(jnp.int32, (tokens, span, width), 1)

    def block(number, carry):
        start = pl.multiple_of(number * tokens, tokens)
        late = (lanes > start + token_of).reshape(tokens * span, width)
        counted = (origin + start + token_of >= back).astype(jnp.float32)
        keys = jnp.stack([sk_ref[pl.ds(start + 1 + i, span), :] for i in range(tokens)])
        values = jnp.stack([sv_ref[pl.ds(start + 1 + i, span), :] for i in range(tokens)])
        for head in range(heads):
            cols = slice(head * width, (head + 1) * width)
            chosen = q32[pl.ds(start, tokens), cols]
            mixed = (chosen[:, None, :] * keys).astype(jnp.bfloat16).reshape(tokens * span, width)
            scores = lax.dot_general(
                mixed, k_ref[...], (((1,), (1,)), ((), ())), preferred_element_type=jnp.float32
            )
            parts = [scores[:, i * width : (i + 1) * width] for i in range(5)]
            parts = [jnp.where(late, parts[0], parts[4])] + parts[1:4]
            top = jnp.maximum(jnp.maximum(parts[0], parts[1]), jnp.maximum(parts[2], parts[3]))
            top = jnp.max(top.reshape(tokens, span, width), axis=1)
            top = jnp.max(top, axis=1, keepdims=True)
            top = jnp.broadcast_to(top[:, :, None], (tokens, span, width))
            top = top.reshape(tokens * span, width)
            weights = [jnp.exp2((p - top) * factor) for p in parts]
            probs = [jnp.where(late, weights[0], 0.0)] + weights[1:]
            probs = probs + [jnp.where(late, 0.0, weights[0])]
            probs = jnp.concatenate([p.astype(jnp.bfloat16) for p in probs], axis=1)
            carried = jnp.dot(probs, v_ref[...], preferred_element_type=jnp.float32)
            above = jnp.sum(carried[:, :width].reshape(tokens, span, width) * values, axis=1)
            below = jnp.sum(carried[:, width:].reshape(tokens, span, width) * counted, axis=1)
            out32[pl.ds(start, tokens), cols] = above / below
        return carry

    steps = rows // tokens // 2
    lax.fori_loop(part * steps, (part + 1) * steps, block, 0)


def rest_kernel(
    place, q_ref, k_ref, v_ref, sk_ref, sv_ref, early_ref, out_ref, q32, out32, *, tokens
):
    half = q_ref.shape[0] // 2
    attend_half(place, q_ref, k_ref, v_ref, sk_ref, sv_ref, q32, out32, tokens, 1)
    out_ref[:half] = early_ref[...]
    out_ref[half:] = out32[half:].astype(jnp.bfloat16)


def attention_call(kernel, operands, out_shape):
    rows, wide = operands[1].shape
    return pl.pallas_call(
        functools.partial(kernel, tokens=16),
        out_shape=out_shape,
        in_specs=[pl.BlockSpec(memory_space=pltpu.SMEM)]
        + [pl.BlockSpec(memory_space=pltpu.VMEM)] * (len(operands) - 1),
        out_specs=jax.tree.map(lambda _: pl.BlockSpec(memory_space=pltpu.VMEM), out_shape),
        scratch_shapes=[
            pltpu.VMEM((rows, wide), jnp.float32),
            pltpu.VMEM((rows, wide), jnp.float32),
        ],
        compiler_params=pltpu.CompilerParams(vmem_limit_bytes=40 * 2**20),
        cost_estimate=pl.CostEstimate(
            flops=10_000_000_000, bytes_accessed=2**20, transcendentals=0
        ),
    )(*operands)


def first_attention(place, q, mine, other):
    rows, wide = q.shape
    width = mine.shape[-1]
    spots = W1 // rows + 1
    shapes = [
        ((rows // 2, wide), jnp.bfloat16),
        ((spots * rows, width), jnp.bfloat16),
        ((spots * rows, 2 * width), jnp.bfloat16),
        ((W2 + rows, width), jnp.float32),
        ((W2 + rows, width), jnp.float32),
    ]
    shapes = [jax.ShapeDtypeStruct(*shape) for shape in shapes]
    early, *window = attention_call(window_kernel, (place, q, mine, other), shapes)
    return early, window


def rest_attention(place, q, window, early):
    return attention_call(
        rest_kernel, (place, q, *window, early), jax.ShapeDtypeStruct(q.shape, jnp.bfloat16)
    )


def pack_kernel(count, *refs):
    own, before, older, out_ref = refs[:4], refs[4], refs[5:-1], refs[-1]
    for to in range(out_ref.shape[0]):
        for kind in range(2):
            line = [ref.at[kind] for ref in older[::-1]] + [before.at[kind], own[kind]]
            for spot, ref in enumerate(line):
                out_ref[to, kind * count + spot] = ref[...]
            out_ref[to, 2 * count + kind] = before[2 + kind]
            out_ref[to, 2 * count + 2 + kind] = own[2 + kind][...]


def pack(own, before, older):
    count = len(older) + 2
    return pl.pallas_call(
        functools.partial(pack_kernel, count),
        out_shape=jax.ShapeDtypeStruct((ZS, 2 * count + 4) + own[0].shape, own[0].dtype),
        in_specs=[pl.BlockSpec(memory_space=pltpu.VMEM)] * (5 + len(older)),
        out_specs=pl.BlockSpec(memory_space=pltpu.VMEM),
    )(*own, before, *older)


def project_kernel(place, *refs):
    tokens, columns, out_ref = refs[:YS], refs[YS : YS + XS], refs[-1]
    x, y, c = place[0], place[1], place[2]
    for d in range(XS):
        to = lax.rem(x + d, XS)
        for e in range(YS):
            slot = lax.rem(y + e + YS - 2 * c, YS)
            total = jnp.dot(tokens[e][0], columns[d][0], preferred_element_type=jnp.float32)
            total += jnp.dot(tokens[e][1], columns[d][1], preferred_element_type=jnp.float32)
            out_ref[slot // 2, to, slot % 2] = total.astype(jnp.bfloat16)


def project(place, tokens, columns):
    rows, wide = tokens[0].shape[1], columns[0].shape[2]
    return pl.pallas_call(
        project_kernel,
        out_shape=jax.ShapeDtypeStruct((2, XS, YS // 2, rows, wide), jnp.bfloat16),
        in_specs=[pl.BlockSpec(memory_space=pltpu.SMEM)]
        + [pl.BlockSpec(memory_space=pltpu.VMEM)] * (XS + YS),
        out_specs=pl.BlockSpec(memory_space=pltpu.VMEM),
        compiler_params=pltpu.CompilerParams(vmem_limit_bytes=40 * 2**20),
        cost_estimate=pl.CostEstimate(
            flops=1_100_000_000, bytes_accessed=4 * 2**20, transcendentals=0
        ),
    )(place, *tokens, *columns)


def in_order(first, second, swap):
    return jnp.where(swap, second, first), jnp.where(swap, first, second)


def per_device(queries, long_keys, long_values, short_keys, short_values, w_out):
    rows = queries.shape[0]
    seq = lax.axis_index("seq")
    head = lax.axis_index("head")
    x, half, y = seq // (HS * YS), seq // YS % HS, seq % YS
    z, c = head // CS, head % CS

    def along(steps):
        def target(x, h, y, z, c):
            to = (h * ZS + z + steps) % (HS * ZS)
            return (x, to // ZS, y, to % ZS, c)

        return target

    def kept_here(h, z):
        return h == z % 2

    def first_up(x, h, y, z, c):
        return along(4)(x, h, y, z, c) if kept_here(h, z) else None

    def first_down(x, h, y, z, c):
        return None if kept_here(h, z) else along(-4)(x, h, y, z, c)

    def second_up(x, h, y, z, c):
        spot = (h * ZS + z - 4) % (HS * ZS)
        return along(4)(x, h, y, z, c) if kept_here(spot // ZS, spot % ZS) else None

    def second_down(x, h, y, z, c):
        spot = (h * ZS + z + 4) % (HS * ZS)
        if kept_here(spot // ZS, spot % ZS):
            return None
        return along(-5 if spot < ZS else -3)(x, h, y, z, c)

    def near(x, h, y, z, c):
        return None if kept_here(h, z) else (x, h, y, z ^ 1, c)

    upward, downward = moved(w_out, first_up), moved(w_out, first_down)

    piece = jnp.stack([long_keys, long_values, short_keys, short_values])
    before = later(piece, 1)
    older = [later(piece[:2], steps) for steps in range(2, W1 // rows + 1)]
    mine = pack((long_keys, long_values, short_keys, short_values), before, older)
    mine, upward, downward = lax.optimization_barrier((mine, upward, downward))
    lines = [[z * CS + core for z in range(ZS)] for core in range(CS)]
    over_z = lax.all_to_all(mine, "head", 0, 0, axis_index_groups=lines, tiled=True)
    over_z, upward, downward = lax.optimization_barrier((over_z, upward, downward))
    over_core = moved(over_z, lambda x, h, y, z, c: (x, h, y, z, 1 - c))
    spot = jnp.stack([seq, c])
    early, window = first_attention(spot, queries, over_z, over_core)
    upward, downward = moved(upward, second_up), moved(downward, second_down)
    beside = moved(w_out, near)

    near_by = half == z % 2
    pair = jnp.stack(
        [jnp.where(near_by, w_out, upward), jnp.where(near_by, beside, downward)]
    )
    pair, early = lax.optimization_barrier((pair, early))
    from_x = [pair] + [
        moved(pair, lambda x, h, y, z, c, d=d: (x - d, h, y, z, c)) for d in (1, 2, 3)
    ]

    attended = rest_attention(spot, queries, window, early)

    beside = moved(attended, lambda x, h, y, z, c: (x, h, y, z ^ 1, c))
    beside, from_x = lax.optimization_barrier((beside, from_x))
    attended = jnp.stack([attended, beside])
    from_y = [attended] + [
        moved(attended, lambda x, h, y, z, c, d=d: (x, h, y - d, z, c)) for d in (1, 2, 3)
    ]
    sums = project(jnp.stack([x, y, c]), from_y, from_x)
    came = moved(sums[1], lambda x, h, y, z, c: (x, h, y, z, 1 - c))
    kept = (sums[0].astype(jnp.float32) + came.astype(jnp.float32)).astype(jnp.bfloat16)
    groups = [
        [(2 * far + low) * CS + core for far in range(ZS // 2)]
        for low in range(2)
        for core in range(CS)
    ]
    parts = lax.all_to_all(kept, "head", 0, 0, axis_index_groups=groups, tiled=True)
    summed = jnp.sum(parts.astype(jnp.float32), axis=0).astype(jnp.bfloat16)
    odd = y % 2 == 1
    sent = in_order(summed[0], summed[1], odd)
    landed = [
        moved(
            sent[j],
            lambda x, h, y, z, c, j=j: (x, h, 2 * c + (j ^ (y % 2)), z, y // 2),
        )
        for j in range(2)
    ]
    return jnp.concatenate(in_order(landed[0], landed[1], odd), axis=1)


def solution(mesh):
    return jax.shard_map(
        per_device,
        mesh=mesh,
        in_specs=(
            P("seq", "head"),
            P(("seq", "head"), None),
            P(("seq", "head"), None),
            P(("seq", "head"), None),
            P(("seq", "head"), None),
            P("head", "seq"),
        ),
        out_specs=P("seq", "head"),
        check_vma=False,
    )
```

```python
import functools
import math

import jax
import jax.numpy as jnp
from jax import lax
from jax.experimental import pallas as pl
from jax.experimental.pallas import tpu as pltpu
from jax.sharding import PartitionSpec as P

W1 = 512
W2 = 32
XS, HS, YS, ZS, CS = 4, 2, 4, 8, 2
BOTH = ("seq", "head")


def seq_of(x, half, y):
    return (x % XS) * HS * YS + (half % HS) * YS + y % YS


def moved(value, target):
    pairs = []
    for x in range(XS):
        for half in range(HS):
            for y in range(YS):
                for z in range(ZS):
                    for c in range(CS):
                        to = target(x, half, y, z, c)
                        if to is None:
                            continue
                        source = seq_of(x, half, y) * ZS * CS + z * CS + c
                        pairs.append((source, seq_of(*to[:3]) * ZS * CS + to[3] * CS + to[4]))
    return lax.ppermute(value, BOTH, pairs)


def later(value, steps):
    count = XS * HS * YS
    return lax.ppermute(value, "seq", [(s, s + steps) for s in range(count - steps)])


def attention_kernel(
    place, q_ref, mine_ref, other_ref, out_ref, k_ref, v_ref, sk_ref, sv_ref, q32, out32, *, tokens
):
    rows, wide = q_ref.shape
    width = k_ref.shape[1]
    heads = wide // width
    block_now, core = place[0], place[1]
    spots = W1 // rows + 1

    def whole(number):
        mine = mine_ref[:, number].astype(jnp.float32)
        other = other_ref[:, number].astype(jnp.float32)
        first, second = jnp.where(core == 1, other, mine), jnp.where(core == 1, mine, other)
        return jnp.concatenate([first[:, None], second[:, None]], axis=1).reshape(rows, width)

    for spot in reversed(range(spots)):
        there = block_now + spot >= spots - 1
        span = pl.ds(spot * rows, rows)
        k_ref[span, :] = whole(spot).astype(jnp.bfloat16)
        v_ref[span, :width] = whole(spots + spot).astype(jnp.bfloat16)
        v_ref[span, width:] = jnp.full((rows, width), jnp.where(there, 1.0, 0.0)).astype(jnp.bfloat16)
    for spot in range(1, spots):

        @pl.when(block_now == spots - 1 - spot)
        def _():
            key = whole(spot)[:1]
            filler = jnp.broadcast_to(key, (spot * rows, width))
            k_ref[: spot * rows, :] = filler.astype(jnp.bfloat16)

    short = whole(2 * spots + 2)
    sk_ref[W2:, :] = short
    edge = whole(2 * spots)[rows - W2 :]
    sk_ref[:W2, :] = jnp.where(block_now == 0, jnp.broadcast_to(short[:1], edge.shape), edge)
    sv_ref[W2:, :] = whole(2 * spots + 3)
    sv_ref[:W2, :] = whole(2 * spots + 1)[rows - W2 :]
    origin = block_now * rows

    span = sk_ref.shape[0] - rows
    factor = 2.5 / math.sqrt(width) * math.log2(math.e)
    q32[...] = q_ref[...].astype(jnp.float32)
    lanes = lax.broadcasted_iota(jnp.int32, (tokens, span, width), 2)
    token_of = lax.broadcasted_iota(jnp.int32, (tokens, span, width), 0)
    back = span - 1 - lax.broadcasted_iota(jnp.int32, (tokens, span, width), 1)

    def block(number, carry):
        start = pl.multiple_of(number * tokens, tokens)
        late = (lanes > start + token_of).reshape(tokens * span, width)
        counted = (origin + start + token_of >= back).astype(jnp.float32)
        keys = jnp.stack([sk_ref[pl.ds(start + 1 + i, span), :] for i in range(tokens)])
        values = jnp.stack([sv_ref[pl.ds(start + 1 + i, span), :] for i in range(tokens)])
        for head in range(heads):
            cols = slice(head * width, (head + 1) * width)
            chosen = q32[pl.ds(start, tokens), cols]
            mixed = (chosen[:, None, :] * keys).astype(jnp.bfloat16).reshape(tokens * span, width)
            scores = lax.dot_general(
                mixed, k_ref[...], (((1,), (1,)), ((), ())), preferred_element_type=jnp.float32
            )
            parts = [scores[:, i * width : (i + 1) * width] for i in range(5)]
            parts = [jnp.where(late, parts[0], parts[4])] + parts[1:4]
            top = jnp.maximum(jnp.maximum(parts[0], parts[1]), jnp.maximum(parts[2], parts[3]))
            top = jnp.max(top.reshape(tokens, span, width), axis=1)
            top = jnp.max(top, axis=1, keepdims=True)
            top = jnp.broadcast_to(top[:, :, None], (tokens, span, width))
            top = top.reshape(tokens * span, width)
            weights = [jnp.exp2((p - top) * factor) for p in parts]
            probs = [jnp.where(late, weights[0], 0.0)] + weights[1:]
            probs = probs + [jnp.where(late, 0.0, weights[0])]
            probs = jnp.concatenate([p.astype(jnp.bfloat16) for p in probs], axis=1)
            carried = jnp.dot(probs, v_ref[...], preferred_element_type=jnp.float32)
            above = jnp.sum(carried[:, :width].reshape(tokens, span, width) * values, axis=1)
            below = jnp.sum(carried[:, width:].reshape(tokens, span, width) * counted, axis=1)
            out32[pl.ds(start, tokens), cols] = above / below
        return carry

    lax.fori_loop(0, rows // tokens, block, 0)
    out_ref[...] = out32[...].astype(jnp.bfloat16)


def attention(place, q, mine, other):
    rows, wide = q.shape
    width = mine.shape[-1]
    spots = W1 // rows + 1
    return pl.pallas_call(
        functools.partial(attention_kernel, tokens=16),
        out_shape=jax.ShapeDtypeStruct((rows, wide), jnp.bfloat16),
        in_specs=[pl.BlockSpec(memory_space=pltpu.SMEM)]
        + [pl.BlockSpec(memory_space=pltpu.VMEM)] * 3,
        out_specs=pl.BlockSpec(memory_space=pltpu.VMEM),
        scratch_shapes=[
            pltpu.VMEM((spots * rows, width), jnp.bfloat16),
            pltpu.VMEM((spots * rows, 2 * width), jnp.bfloat16),
            pltpu.VMEM((W2 + rows, width), jnp.float32),
            pltpu.VMEM((W2 + rows, width), jnp.float32),
            pltpu.VMEM((rows, wide), jnp.float32),
            pltpu.VMEM((rows, wide), jnp.float32),
        ],
        compiler_params=pltpu.CompilerParams(vmem_limit_bytes=40 * 2**20),
        cost_estimate=pl.CostEstimate(
            flops=20_000_000_000, bytes_accessed=2**20, transcendentals=0
        ),
    )(place, q, mine, other)


def pack_kernel(count, *refs):
    own, before, older, out_ref = refs[:4], refs[4], refs[5:-1], refs[-1]
    for to in range(out_ref.shape[0]):
        for kind in range(2):
            line = [ref.at[kind] for ref in older[::-1]] + [before.at[kind], own[kind]]
            for spot, ref in enumerate(line):
                out_ref[to, kind * count + spot] = ref[...]
            out_ref[to, 2 * count + kind] = before[2 + kind]
            out_ref[to, 2 * count + 2 + kind] = own[2 + kind][...]


def pack(own, before, older):
    count = len(older) + 2
    return pl.pallas_call(
        functools.partial(pack_kernel, count),
        out_shape=jax.ShapeDtypeStruct((ZS, 2 * count + 4) + own[0].shape, own[0].dtype),
        in_specs=[pl.BlockSpec(memory_space=pltpu.VMEM)] * (5 + len(older)),
        out_specs=pl.BlockSpec(memory_space=pltpu.VMEM),
    )(*own, before, *older)


def project_kernel(place, *refs):
    tokens, columns, out_ref = refs[:YS], refs[YS : YS + XS], refs[-1]
    x, y, far, c = place[0], place[1], place[2], place[3]
    for d in range(XS):
        to = lax.rem(x + d, XS) ^ far
        for e in range(YS):
            slot = lax.rem(y + e + YS - 2 * c, YS)
            total = jnp.dot(tokens[e][0], columns[d][0], preferred_element_type=jnp.float32)
            total += jnp.dot(tokens[e][1], columns[d][1], preferred_element_type=jnp.float32)
            out_ref[slot // 2, to, slot % 2] = total.astype(jnp.bfloat16)


def project(place, tokens, columns):
    rows, wide = tokens[0].shape[1], columns[0].shape[2]
    return pl.pallas_call(
        project_kernel,
        out_shape=jax.ShapeDtypeStruct((2, XS, YS // 2, rows, wide), jnp.bfloat16),
        in_specs=[pl.BlockSpec(memory_space=pltpu.SMEM)]
        + [pl.BlockSpec(memory_space=pltpu.VMEM)] * (XS + YS),
        out_specs=pl.BlockSpec(memory_space=pltpu.VMEM),
        compiler_params=pltpu.CompilerParams(vmem_limit_bytes=40 * 2**20),
        cost_estimate=pl.CostEstimate(
            flops=1_100_000_000, bytes_accessed=4 * 2**20, transcendentals=0
        ),
    )(place, *tokens, *columns)


def in_order(first, second, swap):
    return jnp.where(swap, second, first), jnp.where(swap, first, second)


def per_device(queries, long_keys, long_values, short_keys, short_values, w_out):
    rows = queries.shape[0]
    seq = lax.axis_index("seq")
    head = lax.axis_index("head")
    x, half, y = seq // (HS * YS), seq // YS % HS, seq % YS
    z, c = head // CS, head % CS

    def along(steps):
        def target(x, h, y, z, c):
            to = (h * ZS + z + steps) % (HS * ZS)
            return (x, to // ZS, y, to % ZS, c)

        return target

    def kept_here(h, z):
        return h == z % 2

    def first_up(x, h, y, z, c):
        return along(4)(x, h, y, z, c) if kept_here(h, z) else None

    def first_down(x, h, y, z, c):
        return None if kept_here(h, z) else along(-4)(x, h, y, z, c)

    def second_up(x, h, y, z, c):
        spot = (h * ZS + z - 4) % (HS * ZS)
        return along(4)(x, h, y, z, c) if kept_here(spot // ZS, spot % ZS) else None

    def second_down(x, h, y, z, c):
        spot = (h * ZS + z + 4) % (HS * ZS)
        if kept_here(spot // ZS, spot % ZS):
            return None
        return along(-5 if spot < ZS else -3)(x, h, y, z, c)

    def near(x, h, y, z, c):
        return None if kept_here(h, z) else (x, h, y, z ^ 1, c)

    upward, downward = moved(w_out, first_up), moved(w_out, first_down)

    piece = jnp.stack([long_keys, long_values, short_keys, short_values])
    before = later(piece, 1)
    older = [later(piece[:2], steps) for steps in range(2, W1 // rows + 1)]
    mine = pack((long_keys, long_values, short_keys, short_values), before, older)
    lines = [[z * CS + core for z in range(ZS)] for core in range(CS)]
    mine, upward, downward = lax.optimization_barrier((mine, upward, downward))
    upward, downward = moved(upward, second_up), moved(downward, second_down)
    beside = moved(w_out, near)
    over_z = lax.all_to_all(mine, "head", 0, 0, axis_index_groups=lines, tiled=True)
    over_core = moved(over_z, lambda x, h, y, z, c: (x, h, y, z, 1 - c))

    near_by = half == z % 2
    pair = jnp.stack(
        [jnp.where(near_by, w_out, upward), jnp.where(near_by, beside, downward)]
    )
    pair, over_core = lax.optimization_barrier((pair, over_core))
    from_x = [pair] + [
        moved(pair, lambda x, h, y, z, c, d=d: (x - d, h, y, z, c)) for d in (1, 2, 3)
    ]

    attended = attention(jnp.stack([seq, c]), queries, over_z, over_core)
    beside = moved(attended, lambda x, h, y, z, c: (x, h, y, z ^ 1, c))
    beside, from_x = lax.optimization_barrier((beside, from_x))
    attended = jnp.stack([attended, beside])
    from_y = [attended] + [
        moved(attended, lambda x, h, y, z, c, d=d: (x, h, y - d, z, c)) for d in (1, 2, 3)
    ]
    sums = project(jnp.stack([x, y, z // 2, c]), from_y, from_x)
    came = moved(sums[1], lambda x, h, y, z, c: (x, h, y, z, 1 - c))
    kept = (sums[0].astype(jnp.float32) + came.astype(jnp.float32)).astype(jnp.bfloat16)
    parts = [kept[0]] + [
        moved(kept[k], lambda x, h, y, z, c, k=k: (x, h, y, z ^ (2 * k), c)) for k in (3, 2, 1)
    ]
    summed = sum(part.astype(jnp.float32) for part in parts).astype(jnp.bfloat16)
    odd = y % 2 == 1
    sent = in_order(summed[0], summed[1], odd)
    landed = [
        moved(
            sent[j],
            lambda x, h, y, z, c, j=j: (x, h, 2 * c + (j ^ (y % 2)), z, y // 2),
        )
        for j in range(2)
    ]
    return jnp.concatenate(in_order(landed[0], landed[1], odd), axis=1)


def solution(mesh):
    return jax.shard_map(
        per_device,
        mesh=mesh,
        in_specs=(
            P("seq", "head"),
            P(("seq", "head"), None),
            P(("seq", "head"), None),
            P(("seq", "head"), None),
            P(("seq", "head"), None),
            P("head", "seq"),
        ),
        out_specs=P("seq", "head"),
        check_vma=False,
    )
```

```python
import functools
import math

import jax
import jax.numpy as jnp
from jax import lax
from jax.experimental import pallas as pl
from jax.experimental.pallas import tpu as pltpu
from jax.sharding import PartitionSpec as P

W1 = 512
W2 = 32
XS, HS, YS, ZS, CS = 4, 2, 4, 8, 2
BOTH = ("seq", "head")


def seq_of(x, half, y):
    return (x % XS) * HS * YS + (half % HS) * YS + y % YS


def moved(value, target):
    pairs = []
    for x in range(XS):
        for half in range(HS):
            for y in range(YS):
                for z in range(ZS):
                    for c in range(CS):
                        to = target(x, half, y, z, c)
                        if to is None:
                            continue
                        source = seq_of(x, half, y) * ZS * CS + z * CS + c
                        pairs.append((source, seq_of(*to[:3]) * ZS * CS + to[3] * CS + to[4]))
    return lax.ppermute(value, BOTH, pairs)


def later(value, steps):
    count = XS * HS * YS
    return lax.ppermute(value, "seq", [(s, s + steps) for s in range(count - steps)])


def attention_kernel(
    place, q_ref, mine_ref, other_ref, out_ref, k_ref, v_ref, sk_ref, sv_ref, q32, out32, *, tokens
):
    rows, wide = q_ref.shape
    width = k_ref.shape[1]
    heads = wide // width
    block_now, core, z = place[0], place[1], place[2]
    spots = W1 // rows + 1

    def spread(ref, number):
        rows_of = []
        for to in range(ZS):
            way = to ^ z
            at = way // 4 + way // 2 % 2 * 2 + way % 2 * 4
            rows_of.append(ref[at, number].astype(jnp.float32))
        return jnp.stack(rows_of)

    def whole(number):
        mine, other = spread(mine_ref, number), spread(other_ref, number)
        first, second = jnp.where(core == 1, other, mine), jnp.where(core == 1, mine, other)
        return jnp.concatenate([first[:, None], second[:, None]], axis=1).reshape(rows, width)

    for spot in reversed(range(spots)):
        there = block_now + spot >= spots - 1
        span = pl.ds(spot * rows, rows)
        k_ref[span, :] = whole(spot).astype(jnp.bfloat16)
        v_ref[span, :width] = whole(spots + spot).astype(jnp.bfloat16)
        v_ref[span, width:] = jnp.full((rows, width), jnp.where(there, 1.0, 0.0)).astype(jnp.bfloat16)
    for spot in range(1, spots):

        @pl.when(block_now == spots - 1 - spot)
        def _():
            key = whole(spot)[:1]
            filler = jnp.broadcast_to(key, (spot * rows, width))
            k_ref[: spot * rows, :] = filler.astype(jnp.bfloat16)

    short = whole(2 * spots + 2)
    sk_ref[W2:, :] = short
    edge = whole(2 * spots)[rows - W2 :]
    sk_ref[:W2, :] = jnp.where(block_now == 0, jnp.broadcast_to(short[:1], edge.shape), edge)
    sv_ref[W2:, :] = whole(2 * spots + 3)
    sv_ref[:W2, :] = whole(2 * spots + 1)[rows - W2 :]
    origin = block_now * rows

    span = sk_ref.shape[0] - rows
    factor = 2.5 / math.sqrt(width) * math.log2(math.e)
    q32[...] = q_ref[...].astype(jnp.float32)
    lanes = lax.broadcasted_iota(jnp.int32, (tokens, span, width), 2)
    token_of = lax.broadcasted_iota(jnp.int32, (tokens, span, width), 0)
    back = span - 1 - lax.broadcasted_iota(jnp.int32, (tokens, span, width), 1)

    def block(number, carry):
        start = pl.multiple_of(number * tokens, tokens)
        late = (lanes > start + token_of).reshape(tokens * span, width)
        counted = (origin + start + token_of >= back).astype(jnp.float32)
        keys = jnp.stack([sk_ref[pl.ds(start + 1 + i, span), :] for i in range(tokens)])
        values = jnp.stack([sv_ref[pl.ds(start + 1 + i, span), :] for i in range(tokens)])
        for head in range(heads):
            cols = slice(head * width, (head + 1) * width)
            chosen = q32[pl.ds(start, tokens), cols]
            mixed = (chosen[:, None, :] * keys).astype(jnp.bfloat16).reshape(tokens * span, width)
            scores = lax.dot_general(
                mixed, k_ref[...], (((1,), (1,)), ((), ())), preferred_element_type=jnp.float32
            )
            parts = [scores[:, i * width : (i + 1) * width] for i in range(5)]
            parts = [jnp.where(late, parts[0], parts[4])] + parts[1:4]
            top = jnp.maximum(jnp.maximum(parts[0], parts[1]), jnp.maximum(parts[2], parts[3]))
            top = jnp.max(top.reshape(tokens, span, width), axis=1)
            top = jnp.max(top, axis=1, keepdims=True)
            top = jnp.broadcast_to(top[:, :, None], (tokens, span, width))
            top = top.reshape(tokens * span, width)
            weights = [jnp.exp2((p - top) * factor) for p in parts]
            probs = [jnp.where(late, weights[0], 0.0)] + weights[1:]
            probs = probs + [jnp.where(late, 0.0, weights[0])]
            probs = jnp.concatenate([p.astype(jnp.bfloat16) for p in probs], axis=1)
            carried = jnp.dot(probs, v_ref[...], preferred_element_type=jnp.float32)
            above = jnp.sum(carried[:, :width].reshape(tokens, span, width) * values, axis=1)
            below = jnp.sum(carried[:, width:].reshape(tokens, span, width) * counted, axis=1)
            out32[pl.ds(start, tokens), cols] = above / below
        return carry

    lax.fori_loop(0, rows // tokens, block, 0)
    out_ref[...] = out32[...].astype(jnp.bfloat16)


def attention(place, q, mine, other):
    rows, wide = q.shape
    width = mine.shape[-1]
    spots = W1 // rows + 1
    return pl.pallas_call(
        functools.partial(attention_kernel, tokens=16),
        out_shape=jax.ShapeDtypeStruct((rows, wide), jnp.bfloat16),
        in_specs=[pl.BlockSpec(memory_space=pltpu.SMEM)]
        + [pl.BlockSpec(memory_space=pltpu.VMEM)] * 3,
        out_specs=pl.BlockSpec(memory_space=pltpu.VMEM),
        scratch_shapes=[
            pltpu.VMEM((spots * rows, width), jnp.bfloat16),
            pltpu.VMEM((spots * rows, 2 * width), jnp.bfloat16),
            pltpu.VMEM((W2 + rows, width), jnp.float32),
            pltpu.VMEM((W2 + rows, width), jnp.float32),
            pltpu.VMEM((rows, wide), jnp.float32),
            pltpu.VMEM((rows, wide), jnp.float32),
        ],
        compiler_params=pltpu.CompilerParams(vmem_limit_bytes=40 * 2**20),
        cost_estimate=pl.CostEstimate(
            flops=20_000_000_000, bytes_accessed=2**20, transcendentals=0
        ),
    )(place, q, mine, other)


def pack_kernel(count, *refs):
    own, before, older, out_ref = refs[:4], refs[4], refs[5:-1], refs[-1]
    for kind in range(2):
        line = [ref.at[kind] for ref in older[::-1]] + [before.at[kind], own[kind]]
        for spot, ref in enumerate(line):
            out_ref[0, kind * count + spot] = ref[...]
        out_ref[0, 2 * count + kind] = before[2 + kind]
        out_ref[0, 2 * count + 2 + kind] = own[2 + kind][...]


def pack(own, before, older):
    count = len(older) + 2
    return pl.pallas_call(
        functools.partial(pack_kernel, count),
        out_shape=jax.ShapeDtypeStruct((1, 2 * count + 4) + own[0].shape, own[0].dtype),
        in_specs=[pl.BlockSpec(memory_space=pltpu.VMEM)] * (5 + len(older)),
        out_specs=pl.BlockSpec(memory_space=pltpu.VMEM),
    )(*own, before, *older)


def project_kernel(place, *refs):
    tokens, columns, out_ref = refs[:YS], refs[YS : YS + XS], refs[-1]
    x, y, far, c = place[0], place[1], place[2], place[3]
    for d in range(XS):
        to = lax.rem(x + d, XS) ^ far
        for e in range(YS):
            slot = lax.rem(y + e + YS - 2 * c, YS)
            total = jnp.dot(tokens[e][0], columns[d][0], preferred_element_type=jnp.float32)
            total += jnp.dot(tokens[e][1], columns[d][1], preferred_element_type=jnp.float32)
            out_ref[slot // 2, to, slot % 2] = total.astype(jnp.bfloat16)


def project(place, tokens, columns):
    rows, wide = tokens[0].shape[1], columns[0].shape[2]
    return pl.pallas_call(
        project_kernel,
        out_shape=jax.ShapeDtypeStruct((2, XS, YS // 2, rows, wide), jnp.bfloat16),
        in_specs=[pl.BlockSpec(memory_space=pltpu.SMEM)]
        + [pl.BlockSpec(memory_space=pltpu.VMEM)] * (XS + YS),
        out_specs=pl.BlockSpec(memory_space=pltpu.VMEM),
        compiler_params=pltpu.CompilerParams(vmem_limit_bytes=40 * 2**20),
        cost_estimate=pl.CostEstimate(
            flops=1_100_000_000, bytes_accessed=4 * 2**20, transcendentals=0
        ),
    )(place, *tokens, *columns)


def in_order(first, second, swap):
    return jnp.where(swap, second, first), jnp.where(swap, first, second)


def per_device(queries, long_keys, long_values, short_keys, short_values, w_out):
    rows = queries.shape[0]
    seq = lax.axis_index("seq")
    head = lax.axis_index("head")
    x, half, y = seq // (HS * YS), seq // YS % HS, seq % YS
    z, c = head // CS, head % CS

    piece = jnp.stack([long_keys, long_values, short_keys, short_values])
    before = later(piece, 1)
    older = [later(piece[:2], steps) for steps in range(2, W1 // rows + 1)]
    held = pack((long_keys, long_values, short_keys, short_values), before, older)
    held, w_out = lax.optimization_barrier((held, w_out))

    first_up = {0: 5, 2: 7, 4: 8, 6: 10, 9: 12, 11: 14, 13: 1, 15: 3}
    second_up = {first_up[spot]: (spot + 8) % 16 for spot in first_up}
    stay = [spot for spot in range(16) if spot not in first_up]
    first_up.update({spot: spot ^ 1 for spot in stay})
    first_down = {spot: (spot - 4) % 16 for spot in stay}
    second_down = {first_down[spot]: (spot ^ 1) ^ 8 for spot in stay}

    def along(table):
        def target(x, h, y, z, c):
            to = table.get(h * ZS + z)
            return None if to is None else (x, to // ZS, y, to % ZS, c)

        return target

    for far in (4, 2, 1):
        if far == 4:
            upward, downward = moved(w_out, along(first_up)), moved(w_out, along(first_down))
        came = moved(held, lambda x, h, y, z, c, far=far: (x, h, y, z ^ far, c))
        held = jnp.concatenate([held, came])
    held, upward, downward = lax.optimization_barrier((held, upward, downward))
    over_core = moved(held, lambda x, h, y, z, c: (x, h, y, z, 1 - c))
    attended = attention(jnp.stack([seq, c, z]), queries, held, over_core)
    long_way, downward = moved(upward, along(second_up)), moved(downward, along(second_down))

    near_by = half == z % 2
    pair = jnp.stack(
        [jnp.where(near_by, w_out, long_way), jnp.where(near_by, upward, downward)]
    )
    pair, attended = lax.optimization_barrier((pair, attended))
    from_x = [pair] + [
        moved(pair, lambda x, h, y, z, c, d=d: (x - d, h, y, z, c)) for d in (1, 2, 3)
    ]

    beside = moved(attended, lambda x, h, y, z, c: (x, h, y, z ^ 1, c))
    attended = jnp.stack([attended, beside])
    from_y = [attended] + [
        moved(attended, lambda x, h, y, z, c, d=d: (x, h, y - d, z, c)) for d in (1, 2, 3)
    ]
    sums = project(jnp.stack([x, y, z // 2, c]), from_y, from_x)
    came = moved(sums[1], lambda x, h, y, z, c: (x, h, y, z, 1 - c))
    kept = (sums[0].astype(jnp.float32) + came.astype(jnp.float32)).astype(jnp.bfloat16)
    parts = [kept[0]] + [
        moved(kept[k], lambda x, h, y, z, c, k=k: (x, h, y, z ^ (2 * k), c)) for k in (3, 2, 1)
    ]
    summed = sum(part.astype(jnp.float32) for part in parts).astype(jnp.bfloat16)
    odd = y % 2 == 1
    sent = in_order(summed[0], summed[1], odd)
    landed = [
        moved(
            sent[j],
            lambda x, h, y, z, c, j=j: (x, h, 2 * c + (j ^ (y % 2)), z, y // 2),
        )
        for j in range(2)
    ]
    return jnp.concatenate(in_order(landed[0], landed[1], odd), axis=1)


def solution(mesh):
    return jax.shard_map(
        per_device,
        mesh=mesh,
        in_specs=(
            P("seq", "head"),
            P(("seq", "head"), None),
            P(("seq", "head"), None),
            P(("seq", "head"), None),
            P(("seq", "head"), None),
            P("head", "seq"),
        ),
        out_specs=P("seq", "head"),
        check_vma=False,
    )
```

```python
import functools
import math

import jax
import jax.numpy as jnp
from jax import lax
from jax.experimental import pallas as pl
from jax.experimental.pallas import tpu as pltpu
from jax.sharding import PartitionSpec as P

W1 = 512
W2 = 32
XS, HS, YS, ZS, CS = 4, 2, 4, 8, 2
BOTH = ("seq", "head")


def seq_of(x, half, y):
    return (x % XS) * HS * YS + (half % HS) * YS + y % YS


def moved(value, target):
    pairs = []
    for x in range(XS):
        for half in range(HS):
            for y in range(YS):
                for z in range(ZS):
                    for c in range(CS):
                        to = target(x, half, y, z, c)
                        if to is None:
                            continue
                        source = seq_of(x, half, y) * ZS * CS + z * CS + c
                        pairs.append((source, seq_of(*to[:3]) * ZS * CS + to[3] * CS + to[4]))
    return lax.ppermute(value, BOTH, pairs)


def later(value, steps):
    count = XS * HS * YS
    return lax.ppermute(value, "seq", [(s, s + steps) for s in range(count - steps)])


def attention_kernel(
    place, q_ref, mine_ref, other_ref, out_ref, k_ref, v_ref, sk_ref, sv_ref, q32, out32, *, tokens
):
    rows, wide = q_ref.shape
    width = k_ref.shape[1]
    heads = wide // width
    block_now, core = place[0], place[1]
    spots = W1 // rows + 1

    def whole(number):
        mine = mine_ref[:, number].astype(jnp.float32)
        other = other_ref[:, number].astype(jnp.float32)
        first, second = jnp.where(core == 1, other, mine), jnp.where(core == 1, mine, other)
        return jnp.concatenate([first[:, None], second[:, None]], axis=1).reshape(rows, width)

    for spot in reversed(range(spots)):
        there = block_now + spot >= spots - 1
        span = pl.ds(spot * rows, rows)
        k_ref[span, :] = whole(spot).astype(jnp.bfloat16)
        v_ref[span, :width] = whole(spots + spot).astype(jnp.bfloat16)
        v_ref[span, width:] = jnp.full((rows, width), jnp.where(there, 1.0, 0.0)).astype(jnp.bfloat16)
    for spot in range(1, spots):

        @pl.when(block_now == spots - 1 - spot)
        def _():
            key = whole(spot)[:1]
            filler = jnp.broadcast_to(key, (spot * rows, width))
            k_ref[: spot * rows, :] = filler.astype(jnp.bfloat16)

    short = whole(2 * spots + 2)
    sk_ref[W2:, :] = short
    edge = whole(2 * spots)[rows - W2 :]
    sk_ref[:W2, :] = jnp.where(block_now == 0, jnp.broadcast_to(short[:1], edge.shape), edge)
    sv_ref[W2:, :] = whole(2 * spots + 3)
    sv_ref[:W2, :] = whole(2 * spots + 1)[rows - W2 :]
    origin = block_now * rows

    span = sk_ref.shape[0] - rows
    factor = 2.5 / math.sqrt(width) * math.log2(math.e)
    q32[...] = q_ref[...].astype(jnp.float32)
    lanes = lax.broadcasted_iota(jnp.int32, (tokens, span, width), 2)
    token_of = lax.broadcasted_iota(jnp.int32, (tokens, span, width), 0)
    back = span - 1 - lax.broadcasted_iota(jnp.int32, (tokens, span, width), 1)

    def block(number, carry):
        start = pl.multiple_of(number * tokens, tokens)
        late = (lanes > start + token_of).reshape(tokens * span, width)
        counted = (origin + start + token_of >= back).astype(jnp.float32)
        keys = jnp.stack([sk_ref[pl.ds(start + 1 + i, span), :] for i in range(tokens)])
        values = jnp.stack([sv_ref[pl.ds(start + 1 + i, span), :] for i in range(tokens)])
        for head in range(heads):
            cols = slice(head * width, (head + 1) * width)
            chosen = q32[pl.ds(start, tokens), cols]
            mixed = (chosen[:, None, :] * keys).astype(jnp.bfloat16).reshape(tokens * span, width)
            scores = lax.dot_general(
                mixed, k_ref[...], (((1,), (1,)), ((), ())), preferred_element_type=jnp.float32
            )
            parts = [scores[:, i * width : (i + 1) * width] for i in range(5)]
            parts = [jnp.where(late, parts[0], parts[4])] + parts[1:4]
            top = jnp.maximum(jnp.maximum(parts[0], parts[1]), jnp.maximum(parts[2], parts[3]))
            top = jnp.max(top.reshape(tokens, span, width), axis=1)
            top = jnp.max(top, axis=1, keepdims=True)
            top = jnp.broadcast_to(top[:, :, None], (tokens, span, width))
            top = top.reshape(tokens * span, width)
            weights = [jnp.exp2((p - top) * factor) for p in parts]
            probs = [jnp.where(late, weights[0], 0.0)] + weights[1:]
            probs = probs + [jnp.where(late, 0.0, weights[0])]
            probs = jnp.concatenate([p.astype(jnp.bfloat16) for p in probs], axis=1)
            carried = jnp.dot(probs, v_ref[...], preferred_element_type=jnp.float32)
            above = jnp.sum(carried[:, :width].reshape(tokens, span, width) * values, axis=1)
            below = jnp.sum(carried[:, width:].reshape(tokens, span, width) * counted, axis=1)
            out32[pl.ds(start, tokens), cols] = above / below
        return carry

    lax.fori_loop(0, rows // tokens, block, 0)
    out_ref[...] = out32[...].astype(jnp.bfloat16)


def attention(place, q, mine, other):
    rows, wide = q.shape
    width = mine.shape[-1]
    spots = W1 // rows + 1
    return pl.pallas_call(
        functools.partial(attention_kernel, tokens=32),
        out_shape=jax.ShapeDtypeStruct((rows, wide), jnp.bfloat16),
        in_specs=[pl.BlockSpec(memory_space=pltpu.SMEM)]
        + [pl.BlockSpec(memory_space=pltpu.VMEM)] * 3,
        out_specs=pl.BlockSpec(memory_space=pltpu.VMEM),
        scratch_shapes=[
            pltpu.VMEM((spots * rows, width), jnp.bfloat16),
            pltpu.VMEM((spots * rows, 2 * width), jnp.bfloat16),
            pltpu.VMEM((W2 + rows, width), jnp.float32),
            pltpu.VMEM((W2 + rows, width), jnp.float32),
            pltpu.VMEM((rows, wide), jnp.float32),
            pltpu.VMEM((rows, wide), jnp.float32),
        ],
        compiler_params=pltpu.CompilerParams(vmem_limit_bytes=40 * 2**20),
        cost_estimate=pl.CostEstimate(
            flops=1000, bytes_accessed=1000, transcendentals=0
        ),
    )(place, q, mine, other)


def pack_kernel(count, *refs):
    own, before, older, out_ref = refs[:4], refs[4], refs[5:-1], refs[-1]
    for to in range(out_ref.shape[0]):
        for kind in range(2):
            line = [ref.at[kind] for ref in older[::-1]] + [before.at[kind], own[kind]]
            for spot, ref in enumerate(line):
                out_ref[to, kind * count + spot] = ref[...]
            out_ref[to, 2 * count + kind] = before[2 + kind]
            out_ref[to, 2 * count + 2 + kind] = own[2 + kind][...]


def pack(own, before, older):
    count = len(older) + 2
    return pl.pallas_call(
        functools.partial(pack_kernel, count),
        out_shape=jax.ShapeDtypeStruct((ZS, 2 * count + 4) + own[0].shape, own[0].dtype),
        in_specs=[pl.BlockSpec(memory_space=pltpu.VMEM)] * (5 + len(older)),
        out_specs=pl.BlockSpec(memory_space=pltpu.VMEM),
    )(*own, before, *older)


def project_kernel(place, *refs):
    tokens, columns, out_ref = refs[:YS], refs[YS : YS + XS], refs[-1]
    x, y, far, c = place[0], place[1], place[2], place[3]
    for d in range(XS):
        to = lax.rem(x + d, XS) ^ far
        for e in range(YS):
            slot = lax.rem(y + e + YS - 2 * c, YS)
            total = jnp.dot(tokens[e][0], columns[d][0], preferred_element_type=jnp.float32)
            total += jnp.dot(tokens[e][1], columns[d][1], preferred_element_type=jnp.float32)
            out_ref[slot // 2, to, slot % 2] = total.astype(jnp.bfloat16)


def project(place, tokens, columns):
    rows, wide = tokens[0].shape[1], columns[0].shape[2]
    return pl.pallas_call(
        project_kernel,
        out_shape=jax.ShapeDtypeStruct((2, XS, YS // 2, rows, wide), jnp.bfloat16),
        in_specs=[pl.BlockSpec(memory_space=pltpu.SMEM)]
        + [pl.BlockSpec(memory_space=pltpu.VMEM)] * (XS + YS),
        out_specs=pl.BlockSpec(memory_space=pltpu.VMEM),
        compiler_params=pltpu.CompilerParams(vmem_limit_bytes=40 * 2**20),
        cost_estimate=pl.CostEstimate(
            flops=1_100_000_000, bytes_accessed=4 * 2**20, transcendentals=0
        ),
    )(place, *tokens, *columns)


def in_order(first, second, swap):
    return jnp.where(swap, second, first), jnp.where(swap, first, second)


def per_device(queries, long_keys, long_values, short_keys, short_values, w_out):
    rows = queries.shape[0]
    seq = lax.axis_index("seq")
    head = lax.axis_index("head")
    x, half, y = seq // (HS * YS), seq // YS % HS, seq % YS
    z, c = head // CS, head % CS

    first_up = {0: 5, 2: 7, 4: 8, 6: 10, 9: 12, 11: 14, 13: 1, 15: 3}
    second_up = {first_up[spot]: (spot + 8) % 16 for spot in first_up}
    stay = [spot for spot in range(16) if spot not in first_up]
    first_up.update({spot: spot ^ 1 for spot in stay})
    first_down = {spot: (spot - 4) % 16 for spot in stay}
    second_down = {first_down[spot]: (spot ^ 1) ^ 8 for spot in stay}

    def along(table):
        def target(x, h, y, z, c):
            to = table.get(h * ZS + z)
            return None if to is None else (x, to // ZS, y, to % ZS, c)

        return target

    upward, downward = moved(w_out, along(first_up)), moved(w_out, along(first_down))

    piece = jnp.stack([long_keys, long_values, short_keys, short_values])
    before = later(piece, 1)
    older = [later(piece[:2], steps) for steps in range(2, W1 // rows + 1)]
    mine = pack((long_keys, long_values, short_keys, short_values), before, older)
    lines = [[z * CS + core for z in range(ZS)] for core in range(CS)]
    long_way, downward = moved(upward, along(second_up)), moved(downward, along(second_down))
    near_by = half == z % 2
    pair = jnp.stack(
        [jnp.where(near_by, w_out, long_way), jnp.where(near_by, upward, downward)]
    )
    mine, pair = lax.optimization_barrier((mine, pair))
    over_z = lax.all_to_all(mine, "head", 0, 0, axis_index_groups=lines, tiled=True)
    over_core = moved(over_z, lambda x, h, y, z, c: (x, h, y, z, 1 - c))

    from_x = [pair] + [
        moved(pair, lambda x, h, y, z, c, d=d: (x - d, h, y, z, c)) for d in (1, 2, 3)
    ]

    attended = attention(jnp.stack([seq, c]), queries, over_z, over_core)
    beside = moved(attended, lambda x, h, y, z, c: (x, h, y, z ^ 1, c))
    beside, from_x = lax.optimization_barrier((beside, from_x))
    attended = jnp.stack([attended, beside])
    from_y = [attended] + [
        moved(attended, lambda x, h, y, z, c, d=d: (x, h, y - d, z, c)) for d in (1, 2, 3)
    ]
    sums = project(jnp.stack([x, y, z // 2, c]), from_y, from_x)
    came = moved(sums[1], lambda x, h, y, z, c: (x, h, y, z, 1 - c))
    kept = (sums[0].astype(jnp.float32) + came.astype(jnp.float32)).astype(jnp.bfloat16)
    parts = [kept[0]] + [
        moved(kept[k], lambda x, h, y, z, c, k=k: (x, h, y, z ^ (2 * k), c)) for k in (3, 2, 1)
    ]
    summed = sum(part.astype(jnp.float32) for part in parts).astype(jnp.bfloat16)
    odd = y % 2 == 1
    sent = in_order(summed[0], summed[1], odd)
    landed = [
        moved(
            sent[j],
            lambda x, h, y, z, c, j=j: (x, h, 2 * c + (j ^ (y % 2)), z, y // 2),
        )
        for j in range(2)
    ]
    return jnp.concatenate(in_order(landed[0], landed[1], odd), axis=1)


def solution(mesh):
    return jax.shard_map(
        per_device,
        mesh=mesh,
        in_specs=(
            P("seq", "head"),
            P(("seq", "head"), None),
            P(("seq", "head"), None),
            P(("seq", "head"), None),
            P(("seq", "head"), None),
            P("head", "seq"),
        ),
        out_specs=P("seq", "head"),
        check_vma=False,
    )
```

```python
import functools
import math

import jax
import jax.numpy as jnp
from jax import lax
from jax.experimental import pallas as pl
from jax.experimental.pallas import tpu as pltpu
from jax.sharding import PartitionSpec as P

W1 = 512
W2 = 32
XS, HS, YS, ZS, CS = 4, 2, 4, 8, 2
BOTH = ("seq", "head")


def seq_of(x, half, y):
    return (x % XS) * HS * YS + (half % HS) * YS + y % YS


def moved(value, target):
    pairs = []
    for x in range(XS):
        for half in range(HS):
            for y in range(YS):
                for z in range(ZS):
                    for c in range(CS):
                        to = target(x, half, y, z, c)
                        if to is None:
                            continue
                        source = seq_of(x, half, y) * ZS * CS + z * CS + c
                        pairs.append((source, seq_of(*to[:3]) * ZS * CS + to[3] * CS + to[4]))
    return lax.ppermute(value, BOTH, pairs)


def later(value, steps):
    count = XS * HS * YS
    return lax.ppermute(value, "seq", [(s, s + steps) for s in range(count - steps)])


def attention_kernel(
    place, q_ref, mine_ref, other_ref, out_ref, k_ref, v_ref, sk_ref, sv_ref, q32, out32, *, tokens
):
    rows, wide = q_ref.shape
    width = k_ref.shape[1]
    heads = wide // width
    block_now, core = place[0], place[1]
    spots = W1 // rows + 1

    def whole(number):
        mine = mine_ref[:, number].astype(jnp.float32)
        other = other_ref[:, number].astype(jnp.float32)
        first, second = jnp.where(core == 1, other, mine), jnp.where(core == 1, mine, other)
        return jnp.concatenate([first[:, None], second[:, None]], axis=1).reshape(rows, width)

    for spot in reversed(range(spots)):
        there = block_now + spot >= spots - 1
        span = pl.ds(spot * rows, rows)
        k_ref[span, :] = whole(spot).astype(jnp.bfloat16)
        v_ref[span, :width] = whole(spots + spot).astype(jnp.bfloat16)
        v_ref[span, width:] = jnp.full((rows, width), jnp.where(there, 1.0, 0.0)).astype(jnp.bfloat16)
    for spot in range(1, spots):

        @pl.when(block_now == spots - 1 - spot)
        def _():
            key = whole(spot)[:1]
            filler = jnp.broadcast_to(key, (spot * rows, width))
            k_ref[: spot * rows, :] = filler.astype(jnp.bfloat16)

    short = whole(2 * spots + 2)
    sk_ref[W2:, :] = short
    edge = whole(2 * spots)[rows - W2 :]
    sk_ref[:W2, :] = jnp.where(block_now == 0, jnp.broadcast_to(short[:1], edge.shape), edge)
    sv_ref[W2:, :] = whole(2 * spots + 3)
    sv_ref[:W2, :] = whole(2 * spots + 1)[rows - W2 :]
    origin = block_now * rows

    span = sk_ref.shape[0] - rows
    factor = 2.5 / math.sqrt(width) * math.log2(math.e)
    q32[...] = q_ref[...].astype(jnp.float32)
    lanes = lax.broadcasted_iota(jnp.int32, (tokens, span, width), 2)
    token_of = lax.broadcasted_iota(jnp.int32, (tokens, span, width), 0)
    back = span - 1 - lax.broadcasted_iota(jnp.int32, (tokens, span, width), 1)

    def block(number, carry):
        start = pl.multiple_of(number * tokens, tokens)
        late = (lanes > start + token_of).reshape(tokens * span, width)
        counted = (origin + start + token_of >= back).astype(jnp.float32)
        keys = jnp.stack([sk_ref[pl.ds(start + 1 + i, span), :] for i in range(tokens)])
        values = jnp.stack([sv_ref[pl.ds(start + 1 + i, span), :] for i in range(tokens)])
        for head in range(heads):
            cols = slice(head * width, (head + 1) * width)
            chosen = q32[pl.ds(start, tokens), cols]
            mixed = (chosen[:, None, :] * keys).astype(jnp.bfloat16).reshape(tokens * span, width)
            scores = lax.dot_general(
                mixed, k_ref[...], (((1,), (1,)), ((), ())), preferred_element_type=jnp.float32
            )
            parts = [scores[:, i * width : (i + 1) * width] for i in range(5)]
            parts = [jnp.where(late, parts[0], parts[4])] + parts[1:4]
            top = jnp.maximum(jnp.maximum(parts[0], parts[1]), jnp.maximum(parts[2], parts[3]))
            top = jnp.max(top.reshape(tokens, span, width), axis=1)
            top = jnp.max(top, axis=1, keepdims=True)
            top = jnp.broadcast_to(top[:, :, None], (tokens, span, width))
            top = top.reshape(tokens * span, width)
            weights = [jnp.exp2((p - top) * factor) for p in parts]
            probs = [jnp.where(late, weights[0], 0.0)] + weights[1:]
            probs = probs + [jnp.where(late, 0.0, weights[0])]
            probs = jnp.concatenate([p.astype(jnp.bfloat16) for p in probs], axis=1)
            carried = jnp.dot(probs, v_ref[...], preferred_element_type=jnp.float32)
            above = jnp.sum(carried[:, :width].reshape(tokens, span, width) * values, axis=1)
            below = jnp.sum(carried[:, width:].reshape(tokens, span, width) * counted, axis=1)
            out32[pl.ds(start, tokens), cols] = above / below
        return carry

    lax.fori_loop(0, rows // tokens, block, 0)
    out_ref[...] = out32[...].astype(jnp.bfloat16)


def attention(place, q, mine, other):
    rows, wide = q.shape
    width = mine.shape[-1]
    spots = W1 // rows + 1
    return pl.pallas_call(
        functools.partial(attention_kernel, tokens=32),
        out_shape=jax.ShapeDtypeStruct((rows, wide), jnp.bfloat16),
        in_specs=[pl.BlockSpec(memory_space=pltpu.SMEM)]
        + [pl.BlockSpec(memory_space=pltpu.VMEM)] * 3,
        out_specs=pl.BlockSpec(memory_space=pltpu.VMEM),
        scratch_shapes=[
            pltpu.VMEM((spots * rows, width), jnp.bfloat16),
            pltpu.VMEM((spots * rows, 2 * width), jnp.bfloat16),
            pltpu.VMEM((W2 + rows, width), jnp.float32),
            pltpu.VMEM((W2 + rows, width), jnp.float32),
            pltpu.VMEM((rows, wide), jnp.float32),
            pltpu.VMEM((rows, wide), jnp.float32),
        ],
        compiler_params=pltpu.CompilerParams(vmem_limit_bytes=40 * 2**20),
        cost_estimate=pl.CostEstimate(
            flops=20_000_000_000, bytes_accessed=2**20, transcendentals=0
        ),
    )(place, q, mine, other)


def pack_kernel(count, *refs):
    own, before, older, out_ref = refs[:4], refs[4], refs[5:-1], refs[-1]
    for to in range(out_ref.shape[0]):
        for kind in range(2):
            line = [ref.at[kind] for ref in older[::-1]] + [before.at[kind], own[kind]]
            for spot, ref in enumerate(line):
                out_ref[to, kind * count + spot] = ref[...]
            out_ref[to, 2 * count + kind] = before[2 + kind]
            out_ref[to, 2 * count + 2 + kind] = own[2 + kind][...]


def pack(own, before, older):
    count = len(older) + 2
    return pl.pallas_call(
        functools.partial(pack_kernel, count),
        out_shape=jax.ShapeDtypeStruct((ZS, 2 * count + 4) + own[0].shape, own[0].dtype),
        in_specs=[pl.BlockSpec(memory_space=pltpu.VMEM)] * (5 + len(older)),
        out_specs=pl.BlockSpec(memory_space=pltpu.VMEM),
    )(*own, before, *older)


def project_kernel(place, *refs):
    own, beside, columns = refs[:YS], refs[YS : 2 * YS], refs[2 * YS : 2 * YS + XS]
    kept_ref, away_ref = refs[-2:]
    x, y, far, c = place[0], place[1], place[2], place[3]
    for d in range(XS):
        to = lax.rem(x + d, XS) ^ far
        for e in range(YS):
            slot = lax.rem(y + e + YS - 2 * c, YS)
            total = jnp.dot(own[e][...], columns[d][0], preferred_element_type=jnp.float32)
            total += jnp.dot(beside[e][...], columns[d][1], preferred_element_type=jnp.float32)
            total = total.astype(jnp.bfloat16)

            @pl.when(slot < YS // 2)
            def _():
                kept_ref[to, slot % 2] = total

            @pl.when(slot >= YS // 2)
            def _():
                away_ref[to, slot % 2] = total


def small_call(kernel, place, operands, shapes):
    out_shape = [jax.ShapeDtypeStruct(shape, jnp.bfloat16) for shape in shapes]
    return pl.pallas_call(
        kernel,
        out_shape=out_shape,
        in_specs=[pl.BlockSpec(memory_space=pltpu.SMEM)]
        + [pl.BlockSpec(memory_space=pltpu.VMEM)] * len(operands),
        out_specs=[pl.BlockSpec(memory_space=pltpu.VMEM)] * len(shapes),
        compiler_params=pltpu.CompilerParams(vmem_limit_bytes=40 * 2**20),
    )(place, *operands)


def join_kernel(place, kept_ref, came_ref, *out_refs):
    for k, out_ref in enumerate(out_refs):
        total = kept_ref[k].astype(jnp.float32) + came_ref[k].astype(jnp.float32)
        out_ref[...] = total.astype(jnp.bfloat16)


def sum_kernel(place, *refs):
    parts, out_refs = refs[:-2], refs[-2:]
    for number in range(2):
        total = sum(part[number].astype(jnp.float32) for part in parts).astype(jnp.bfloat16)
        swap = place[1] % 2 == 1

        @pl.when(swap)
        def _():
            out_refs[1 - number][...] = total

        @pl.when(jnp.logical_not(swap))
        def _():
            out_refs[number][...] = total


def lay_kernel(place, first_ref, second_ref, out_ref):
    half = first_ref.shape[1]
    swap = place[1] % 2 == 1

    @pl.when(swap)
    def _():
        out_ref[:, :half] = second_ref[...]
        out_ref[:, half:] = first_ref[...]

    @pl.when(jnp.logical_not(swap))
    def _():
        out_ref[:, :half] = first_ref[...]
        out_ref[:, half:] = second_ref[...]


def per_device(queries, long_keys, long_values, short_keys, short_values, w_out):
    rows = queries.shape[0]
    seq = lax.axis_index("seq")
    head = lax.axis_index("head")
    x, half, y = seq // (HS * YS), seq // YS % HS, seq % YS
    z, c = head // CS, head % CS

    def along(steps):
        def target(x, h, y, z, c):
            to = (h * ZS + z + steps) % (HS * ZS)
            return (x, to // ZS, y, to % ZS, c)

        return target

    def kept_here(h, z):
        return h == z % 2

    def first_up(x, h, y, z, c):
        return along(4)(x, h, y, z, c) if kept_here(h, z) else None

    def first_down(x, h, y, z, c):
        return None if kept_here(h, z) else along(-4)(x, h, y, z, c)

    def second_up(x, h, y, z, c):
        spot = (h * ZS + z - 4) % (HS * ZS)
        return along(4)(x, h, y, z, c) if kept_here(spot // ZS, spot % ZS) else None

    def second_down(x, h, y, z, c):
        spot = (h * ZS + z + 4) % (HS * ZS)
        if kept_here(spot // ZS, spot % ZS):
            return None
        return along(-5 if spot < ZS else -3)(x, h, y, z, c)

    def near(x, h, y, z, c):
        return None if kept_here(h, z) else (x, h, y, z ^ 1, c)

    upward, downward = moved(w_out, first_up), moved(w_out, first_down)

    piece = jnp.stack([long_keys, long_values, short_keys, short_values])
    before = later(piece, 1)
    older = [later(piece[:2], steps) for steps in range(2, W1 // rows + 1)]
    mine = pack((long_keys, long_values, short_keys, short_values), before, older)
    lines = [[z * CS + core for z in range(ZS)] for core in range(CS)]
    mine, upward, downward = lax.optimization_barrier((mine, upward, downward))
    upward, downward = moved(upward, second_up), moved(downward, second_down)
    beside = moved(w_out, near)
    over_z = lax.all_to_all(mine, "head", 0, 0, axis_index_groups=lines, tiled=True)
    over_core = moved(over_z, lambda x, h, y, z, c: (x, h, y, z, 1 - c))

    near_by = half == z % 2
    pair = jnp.stack(
        [jnp.where(near_by, w_out, upward), jnp.where(near_by, beside, downward)]
    )
    pair, over_core = lax.optimization_barrier((pair, over_core))
    from_x = [pair] + [
        moved(pair, lambda x, h, y, z, c, d=d: (x - d, h, y, z, c)) for d in (1, 2, 3)
    ]

    attended = attention(jnp.stack([seq, c]), queries, over_z, over_core)
    beside = [
        moved(attended, lambda x, h, y, z, c, d=d: (x, h, y - d, z ^ 1, c)) for d in range(YS)
    ]
    attended, from_x = lax.optimization_barrier((attended, from_x))
    own = [attended] + [
        moved(attended, lambda x, h, y, z, c, d=d: (x, h, y - d, z, c)) for d in (1, 2, 3)
    ]
    place = jnp.stack([x, y, z // 2, c])
    wide = w_out.shape[1]
    block = (YS // 2, rows, wide)
    kept, away = small_call(
        project_kernel, place, own + beside + from_x, [(XS,) + block, (XS,) + block]
    )
    came = moved(away, lambda x, h, y, z, c: (x, h, y, z, 1 - c))
    kept = small_call(join_kernel, place, [kept, came], [block] * XS)
    parts = [kept[0]] + [
        moved(kept[k], lambda x, h, y, z, c, k=k: (x, h, y, z ^ (2 * k), c)) for k in (3, 2, 1)
    ]
    sent = small_call(sum_kernel, place, parts, [(rows, wide)] * 2)
    landed = [
        moved(
            sent[j],
            lambda x, h, y, z, c, j=j: (x, h, 2 * c + (j ^ (y % 2)), z, y // 2),
        )
        for j in range(2)
    ]
    return small_call(lay_kernel, place, landed, [(rows, 2 * wide)])[0]


def solution(mesh):
    return jax.shard_map(
        per_device,
        mesh=mesh,
        in_specs=(
            P("seq", "head"),
            P(("seq", "head"), None),
            P(("seq", "head"), None),
            P(("seq", "head"), None),
            P(("seq", "head"), None),
            P("head", "seq"),
        ),
        out_specs=P("seq", "head"),
        check_vma=False,
    )
```

```python
import functools
import math

import jax
import jax.numpy as jnp
from jax import lax
from jax.experimental import pallas as pl
from jax.experimental.pallas import tpu as pltpu
from jax.sharding import PartitionSpec as P

W1 = 512
W2 = 32
XS, HS, YS, ZS, CS = 4, 2, 4, 8, 2
BOTH = ("seq", "head")


def seq_of(x, half, y):
    return (x % XS) * HS * YS + (half % HS) * YS + y % YS


def moved(value, target):
    pairs = []
    for x in range(XS):
        for half in range(HS):
            for y in range(YS):
                for z in range(ZS):
                    for c in range(CS):
                        to = target(x, half, y, z, c)
                        if to is None:
                            continue
                        source = seq_of(x, half, y) * ZS * CS + z * CS + c
                        pairs.append((source, seq_of(*to[:3]) * ZS * CS + to[3] * CS + to[4]))
    return lax.ppermute(value, BOTH, pairs)


def later(value, steps):
    count = XS * HS * YS
    return lax.ppermute(value, "seq", [(s, s + steps) for s in range(count - steps)])


def attention_kernel(
    place, q_ref, mine_ref, other_ref, out_ref, k_ref, v_ref, sk_ref, sv_ref, q32, out32, *, tokens
):
    rows, wide = q_ref.shape
    width = k_ref.shape[1]
    heads = wide // width
    block_now, core = place[0], place[1]
    spots = W1 // rows + 1

    def whole(number):
        mine = mine_ref[:, number].astype(jnp.float32)
        other = other_ref[:, number].astype(jnp.float32)
        first, second = jnp.where(core == 1, other, mine), jnp.where(core == 1, mine, other)
        return jnp.concatenate([first[:, None], second[:, None]], axis=1).reshape(rows, width)

    for spot in reversed(range(spots)):
        there = block_now + spot >= spots - 1
        span = pl.ds(spot * rows, rows)
        k_ref[span, :] = whole(spot).astype(jnp.bfloat16)
        v_ref[span, :width] = whole(spots + spot).astype(jnp.bfloat16)
        v_ref[span, width:] = jnp.full((rows, width), jnp.where(there, 1.0, 0.0)).astype(jnp.bfloat16)
    for spot in range(1, spots):

        @pl.when(block_now == spots - 1 - spot)
        def _():
            key = whole(spot)[:1]
            filler = jnp.broadcast_to(key, (spot * rows, width))
            k_ref[: spot * rows, :] = filler.astype(jnp.bfloat16)

    short = whole(2 * spots + 2)
    sk_ref[W2:, :] = short
    edge = whole(2 * spots)[rows - W2 :]
    sk_ref[:W2, :] = jnp.where(block_now == 0, jnp.broadcast_to(short[:1], edge.shape), edge)
    sv_ref[W2:, :] = whole(2 * spots + 3)
    sv_ref[:W2, :] = whole(2 * spots + 1)[rows - W2 :]
    origin = block_now * rows

    span = sk_ref.shape[0] - rows
    factor = 2.5 / math.sqrt(width) * math.log2(math.e)
    q32[...] = q_ref[...].astype(jnp.float32)
    lanes = lax.broadcasted_iota(jnp.int32, (tokens, span, width), 2)
    token_of = lax.broadcasted_iota(jnp.int32, (tokens, span, width), 0)
    back = span - 1 - lax.broadcasted_iota(jnp.int32, (tokens, span, width), 1)

    def block(number, carry):
        start = pl.multiple_of(number * tokens, tokens)
        late = (lanes > start + token_of).reshape(tokens * span, width)
        counted = (origin + start + token_of >= back).astype(jnp.float32)
        keys = jnp.stack([sk_ref[pl.ds(start + 1 + i, span), :] for i in range(tokens)])
        values = jnp.stack([sv_ref[pl.ds(start + 1 + i, span), :] for i in range(tokens)])
        for head in range(heads):
            cols = slice(head * width, (head + 1) * width)
            chosen = q32[pl.ds(start, tokens), cols]
            mixed = (chosen[:, None, :] * keys).astype(jnp.bfloat16).reshape(tokens * span, width)
            scores = lax.dot_general(
                mixed, k_ref[...], (((1,), (1,)), ((), ())), preferred_element_type=jnp.float32
            )
            parts = [scores[:, i * width : (i + 1) * width] for i in range(5)]
            parts = [jnp.where(late, parts[0], parts[4])] + parts[1:4]
            top = jnp.maximum(jnp.maximum(parts[0], parts[1]), jnp.maximum(parts[2], parts[3]))
            top = jnp.max(top.reshape(tokens, span, width), axis=1)
            top = jnp.max(top, axis=1, keepdims=True)
            top = jnp.broadcast_to(top[:, :, None], (tokens, span, width))
            top = top.reshape(tokens * span, width)
            weights = [jnp.exp2((p - top) * factor) for p in parts]
            probs = [jnp.where(late, weights[0], 0.0)] + weights[1:]
            probs = probs + [jnp.where(late, 0.0, weights[0])]
            probs = jnp.concatenate([p.astype(jnp.bfloat16) for p in probs], axis=1)
            carried = jnp.dot(probs, v_ref[...], preferred_element_type=jnp.float32)
            above = jnp.sum(carried[:, :width].reshape(tokens, span, width) * values, axis=1)
            below = jnp.sum(carried[:, width:].reshape(tokens, span, width) * counted, axis=1)
            out32[pl.ds(start, tokens), cols] = above / below
        return carry

    lax.fori_loop(0, rows // tokens, block, 0)
    out_ref[...] = out32[...].astype(jnp.bfloat16)


def attention(place, q, mine, other):
    rows, wide = q.shape
    width = mine.shape[-1]
    spots = W1 // rows + 1
    return pl.pallas_call(
        functools.partial(attention_kernel, tokens=32),
        out_shape=jax.ShapeDtypeStruct((rows, wide), jnp.bfloat16),
        in_specs=[pl.BlockSpec(memory_space=pltpu.SMEM)]
        + [pl.BlockSpec(memory_space=pltpu.VMEM)] * 3,
        out_specs=pl.BlockSpec(memory_space=pltpu.VMEM),
        scratch_shapes=[
            pltpu.VMEM((spots * rows, width), jnp.bfloat16),
            pltpu.VMEM((spots * rows, 2 * width), jnp.bfloat16),
            pltpu.VMEM((W2 + rows, width), jnp.float32),
            pltpu.VMEM((W2 + rows, width), jnp.float32),
            pltpu.VMEM((rows, wide), jnp.float32),
            pltpu.VMEM((rows, wide), jnp.float32),
        ],
        compiler_params=pltpu.CompilerParams(vmem_limit_bytes=40 * 2**20),
        cost_estimate=pl.CostEstimate(
            flops=20_000_000_000, bytes_accessed=2**20, transcendentals=0
        ),
    )(place, q, mine, other)


def pack_kernel(count, *refs):
    own, before, older, out_ref = refs[:4], refs[4], refs[5:-1], refs[-1]
    for to in range(out_ref.shape[0]):
        for kind in range(2):
            line = [ref.at[kind] for ref in older[::-1]] + [before.at[kind], own[kind]]
            for spot, ref in enumerate(line):
                out_ref[to, kind * count + spot] = ref[...]
            out_ref[to, 2 * count + kind] = before[2 + kind]
            out_ref[to, 2 * count + 2 + kind] = own[2 + kind][...]


def pack(own, before, older):
    count = len(older) + 2
    return pl.pallas_call(
        functools.partial(pack_kernel, count),
        out_shape=jax.ShapeDtypeStruct((ZS, 2 * count + 4) + own[0].shape, own[0].dtype),
        in_specs=[pl.BlockSpec(memory_space=pltpu.VMEM)] * (5 + len(older)),
        out_specs=pl.BlockSpec(memory_space=pltpu.VMEM),
    )(*own, before, *older)


def project_kernel(place, *refs):
    tokens, columns, out_ref = refs[:YS], refs[YS : YS + XS], refs[-1]
    x, y, far, c = place[0], place[1], place[2], place[3]
    for d in range(XS):
        to = lax.rem(x + d, XS) ^ far
        for e in range(YS):
            slot = lax.rem(y + e + YS - 2 * c, YS)
            total = jnp.dot(tokens[e][0], columns[d][0], preferred_element_type=jnp.float32)
            total += jnp.dot(tokens[e][1], columns[d][1], preferred_element_type=jnp.float32)
            out_ref[slot // 2, to, slot % 2] = total.astype(jnp.bfloat16)


def project(place, tokens, columns):
    rows, wide = tokens[0].shape[1], columns[0].shape[2]
    return pl.pallas_call(
        project_kernel,
        out_shape=jax.ShapeDtypeStruct((2, XS, YS // 2, rows, wide), jnp.bfloat16),
        in_specs=[pl.BlockSpec(memory_space=pltpu.SMEM)]
        + [pl.BlockSpec(memory_space=pltpu.VMEM)] * (XS + YS),
        out_specs=pl.BlockSpec(memory_space=pltpu.VMEM),
        compiler_params=pltpu.CompilerParams(vmem_limit_bytes=40 * 2**20),
        cost_estimate=pl.CostEstimate(
            flops=1_100_000_000, bytes_accessed=4 * 2**20, transcendentals=0
        ),
    )(place, *tokens, *columns)


def in_order(first, second, swap):
    return jnp.where(swap, second, first), jnp.where(swap, first, second)


def per_device(queries, long_keys, long_values, short_keys, short_values, w_out):
    rows = queries.shape[0]
    seq = lax.axis_index("seq")
    head = lax.axis_index("head")
    x, half, y = seq // (HS * YS), seq // YS % HS, seq % YS
    z, c = head // CS, head % CS

    first_up = {0: 5, 2: 7, 4: 8, 6: 10, 9: 12, 11: 14, 13: 1, 15: 3}
    second_up = {first_up[spot]: (spot + 8) % 16 for spot in first_up}
    stay = [spot for spot in range(16) if spot not in first_up]
    first_up.update({spot: spot ^ 1 for spot in stay})
    first_down = {spot: (spot - 4) % 16 for spot in stay}
    second_down = {first_down[spot]: (spot ^ 1) ^ 8 for spot in stay}

    def along(table):
        def target(x, h, y, z, c):
            to = table.get(h * ZS + z)
            return None if to is None else (x, to // ZS, y, to % ZS, c)

        return target

    upward, downward = moved(w_out, along(first_up)), moved(w_out, along(first_down))

    piece = jnp.stack([long_keys, long_values, short_keys, short_values])
    before = later(piece, 1)
    older = [later(piece[:2], steps) for steps in range(2, W1 // rows + 1)]
    mine = pack((long_keys, long_values, short_keys, short_values), before, older)
    lines = [[z * CS + core for z in range(ZS)] for core in range(CS)]
    mine, upward, downward = lax.optimization_barrier((mine, upward, downward))
    long_way, downward = moved(upward, along(second_up)), moved(downward, along(second_down))
    over_z = lax.all_to_all(mine, "head", 0, 0, axis_index_groups=lines, tiled=True)
    over_core = moved(over_z, lambda x, h, y, z, c: (x, h, y, z, 1 - c))

    near_by = half == z % 2
    pair = jnp.stack(
        [jnp.where(near_by, w_out, long_way), jnp.where(near_by, upward, downward)]
    )
    pair, over_core = lax.optimization_barrier((pair, over_core))
    from_x = [pair] + [
        moved(pair, lambda x, h, y, z, c, d=d: (x - d, h, y, z, c)) for d in (1, 2, 3)
    ]

    attended = attention(jnp.stack([seq, c]), queries, over_z, over_core)
    beside = moved(attended, lambda x, h, y, z, c: (x, h, y, z ^ 1, c))
    beside, from_x = lax.optimization_barrier((beside, from_x))
    attended = jnp.stack([attended, beside])
    from_y = [attended] + [
        moved(attended, lambda x, h, y, z, c, d=d: (x, h, y - d, z, c)) for d in (1, 2, 3)
    ]
    sums = project(jnp.stack([x, y, z // 2, c]), from_y, from_x)
    came = moved(sums[1], lambda x, h, y, z, c: (x, h, y, z, 1 - c))
    kept = (sums[0].astype(jnp.float32) + came.astype(jnp.float32)).astype(jnp.bfloat16)
    parts = [kept[0]] + [
        moved(kept[k], lambda x, h, y, z, c, k=k: (x, h, y, z ^ (2 * k), c)) for k in (3, 2, 1)
    ]
    summed = sum(part.astype(jnp.float32) for part in parts).astype(jnp.bfloat16)
    odd = y % 2 == 1
    sent = in_order(summed[0], summed[1], odd)
    landed = [
        moved(
            sent[j],
            lambda x, h, y, z, c, j=j: (x, h, 2 * c + (j ^ (y % 2)), z, y // 2),
        )
        for j in range(2)
    ]
    return jnp.concatenate(in_order(landed[0], landed[1], odd), axis=1)


def solution(mesh):
    return jax.shard_map(
        per_device,
        mesh=mesh,
        in_specs=(
            P("seq", "head"),
            P(("seq", "head"), None),
            P(("seq", "head"), None),
            P(("seq", "head"), None),
            P(("seq", "head"), None),
            P("head", "seq"),
        ),
        out_specs=P("seq", "head"),
        check_vma=False,
    )
```

```python
import functools
import math

import jax
import jax.numpy as jnp
from jax import lax
from jax.experimental import pallas as pl
from jax.experimental.pallas import tpu as pltpu
from jax.sharding import PartitionSpec as P

W1 = 512
W2 = 32
XS, HS, YS, ZS, CS = 4, 2, 4, 8, 2
BOTH = ("seq", "head")


def seq_of(x, half, y):
    return (x % XS) * HS * YS + (half % HS) * YS + y % YS


def moved(value, target):
    pairs = []
    for x in range(XS):
        for half in range(HS):
            for y in range(YS):
                for z in range(ZS):
                    for c in range(CS):
                        to = target(x, half, y, z, c)
                        if to is None:
                            continue
                        source = seq_of(x, half, y) * ZS * CS + z * CS + c
                        pairs.append((source, seq_of(*to[:3]) * ZS * CS + to[3] * CS + to[4]))
    return lax.ppermute(value, BOTH, pairs)


def later(value, steps):
    count = XS * HS * YS
    return lax.ppermute(value, "seq", [(s, s + steps) for s in range(count - steps)])


def attention_kernel(
    place, q_ref, mine_ref, other_ref, out_ref, k_ref, v_ref, sk_ref, sv_ref, q32, out32, *, tokens
):
    rows, wide = q_ref.shape
    width = k_ref.shape[1]
    heads = wide // width
    block_now, core = place[0], place[1]
    spots = W1 // rows + 1

    def whole(number):
        mine = mine_ref[:, number].astype(jnp.float32)
        other = other_ref[:, number].astype(jnp.float32)
        first, second = jnp.where(core == 1, other, mine), jnp.where(core == 1, mine, other)
        return jnp.concatenate([first[:, None], second[:, None]], axis=1).reshape(rows, width)

    for spot in reversed(range(spots)):
        there = block_now + spot >= spots - 1
        span = pl.ds(spot * rows, rows)
        k_ref[span, :] = whole(spot).astype(jnp.bfloat16)
        v_ref[span, :width] = whole(spots + spot).astype(jnp.bfloat16)
        v_ref[span, width:] = jnp.full((rows, width), jnp.where(there, 1.0, 0.0)).astype(jnp.bfloat16)
    for spot in range(1, spots):

        @pl.when(block_now == spots - 1 - spot)
        def _():
            key = whole(spot)[:1]
            filler = jnp.broadcast_to(key, (spot * rows, width))
            k_ref[: spot * rows, :] = filler.astype(jnp.bfloat16)

    short = whole(2 * spots + 2)
    sk_ref[W2:, :] = short
    edge = whole(2 * spots)[rows - W2 :]
    sk_ref[:W2, :] = jnp.where(block_now == 0, jnp.broadcast_to(short[:1], edge.shape), edge)
    sv_ref[W2:, :] = whole(2 * spots + 3)
    sv_ref[:W2, :] = whole(2 * spots + 1)[rows - W2 :]
    origin = block_now * rows

    span = sk_ref.shape[0] - rows
    factor = 2.5 / math.sqrt(width) * math.log2(math.e)
    q32[...] = q_ref[...].astype(jnp.float32)
    lanes = lax.broadcasted_iota(jnp.int32, (tokens, span, width), 2)
    token_of = lax.broadcasted_iota(jnp.int32, (tokens, span, width), 0)
    back = span - 1 - lax.broadcasted_iota(jnp.int32, (tokens, span, width), 1)

    def block(number, carry):
        start = pl.multiple_of(number * tokens, tokens)
        late = (lanes > start + token_of).reshape(tokens * span, width)
        counted = (origin + start + token_of >= back).astype(jnp.float32)
        keys = jnp.stack([sk_ref[pl.ds(start + 1 + i, span), :] for i in range(tokens)])
        values = jnp.stack([sv_ref[pl.ds(start + 1 + i, span), :] for i in range(tokens)])
        for head in range(heads):
            cols = slice(head * width, (head + 1) * width)
            chosen = q32[pl.ds(start, tokens), cols]
            mixed = (chosen[:, None, :] * keys).astype(jnp.bfloat16).reshape(tokens * span, width)
            scores = lax.dot_general(
                mixed, k_ref[...], (((1,), (1,)), ((), ())), preferred_element_type=jnp.float32
            )
            parts = [scores[:, i * width : (i + 1) * width] for i in range(5)]
            parts = [jnp.where(late, parts[0], parts[4])] + parts[1:4]
            top = jnp.maximum(jnp.maximum(parts[0], parts[1]), jnp.maximum(parts[2], parts[3]))
            top = jnp.max(top.reshape(tokens, span, width), axis=1)
            top = jnp.max(top, axis=1, keepdims=True)
            top = jnp.broadcast_to(top[:, :, None], (tokens, span, width))
            top = top.reshape(tokens * span, width)
            weights = [jnp.exp2((p - top) * factor) for p in parts]
            probs = [jnp.where(late, weights[0], 0.0)] + weights[1:]
            probs = probs + [jnp.where(late, 0.0, weights[0])]
            probs = jnp.concatenate([p.astype(jnp.bfloat16) for p in probs], axis=1)
            carried = jnp.dot(probs, v_ref[...], preferred_element_type=jnp.float32)
            above = jnp.sum(carried[:, :width].reshape(tokens, span, width) * values, axis=1)
            below = jnp.sum(carried[:, width:].reshape(tokens, span, width) * counted, axis=1)
            out32[pl.ds(start, tokens), cols] = above / below
        return carry

    lax.fori_loop(0, rows // tokens, block, 0)
    out_ref[...] = out32[...].astype(jnp.bfloat16)


def attention(place, q, mine, other):
    rows, wide = q.shape
    width = mine.shape[-1]
    spots = W1 // rows + 1
    return pl.pallas_call(
        functools.partial(attention_kernel, tokens=32),
        out_shape=jax.ShapeDtypeStruct((rows, wide), jnp.bfloat16),
        in_specs=[pl.BlockSpec(memory_space=pltpu.SMEM)]
        + [pl.BlockSpec(memory_space=pltpu.VMEM)] * 3,
        out_specs=pl.BlockSpec(memory_space=pltpu.VMEM),
        scratch_shapes=[
            pltpu.VMEM((spots * rows, width), jnp.bfloat16),
            pltpu.VMEM((spots * rows, 2 * width), jnp.bfloat16),
            pltpu.VMEM((W2 + rows, width), jnp.float32),
            pltpu.VMEM((W2 + rows, width), jnp.float32),
            pltpu.VMEM((rows, wide), jnp.float32),
            pltpu.VMEM((rows, wide), jnp.float32),
        ],
        compiler_params=pltpu.CompilerParams(vmem_limit_bytes=40 * 2**20),
        cost_estimate=pl.CostEstimate(
            flops=20_000_000_000, bytes_accessed=2**20, transcendentals=0
        ),
    )(place, q, mine, other)


def pack_kernel(count, *refs):
    own, before, older, out_ref = refs[:4], refs[4], refs[5:-1], refs[-1]
    for to in range(out_ref.shape[0]):
        for kind in range(2):
            line = [ref.at[kind] for ref in older[::-1]] + [before.at[kind], own[kind]]
            for spot, ref in enumerate(line):
                out_ref[to, kind * count + spot] = ref[...]
            out_ref[to, 2 * count + kind] = before[2 + kind]
            out_ref[to, 2 * count + 2 + kind] = own[2 + kind][...]


def pack(own, before, older):
    count = len(older) + 2
    return pl.pallas_call(
        functools.partial(pack_kernel, count),
        out_shape=jax.ShapeDtypeStruct((ZS, 2 * count + 4) + own[0].shape, own[0].dtype),
        in_specs=[pl.BlockSpec(memory_space=pltpu.VMEM)] * (5 + len(older)),
        out_specs=pl.BlockSpec(memory_space=pltpu.VMEM),
    )(*own, before, *older)


def project_kernel(place, *refs):
    tokens, columns, out_ref = refs[:YS], refs[YS : YS + XS], refs[-1]
    x, y, far, c = place[0], place[1], place[2], place[3]
    for d in range(XS):
        to = lax.rem(x + d, XS) ^ far
        for e in range(YS):
            slot = lax.rem(y + e + YS - 2 * c, YS)
            total = jnp.dot(tokens[e][0], columns[d][0], preferred_element_type=jnp.float32)
            total += jnp.dot(tokens[e][1], columns[d][1], preferred_element_type=jnp.float32)
            out_ref[slot // 2, to, slot % 2] = total.astype(jnp.bfloat16)


def project(place, tokens, columns):
    rows, wide = tokens[0].shape[1], columns[0].shape[2]
    return pl.pallas_call(
        project_kernel,
        out_shape=jax.ShapeDtypeStruct((2, XS, YS // 2, rows, wide), jnp.bfloat16),
        in_specs=[pl.BlockSpec(memory_space=pltpu.SMEM)]
        + [pl.BlockSpec(memory_space=pltpu.VMEM)] * (XS + YS),
        out_specs=pl.BlockSpec(memory_space=pltpu.VMEM),
        compiler_params=pltpu.CompilerParams(vmem_limit_bytes=40 * 2**20),
        cost_estimate=pl.CostEstimate(
            flops=1_100_000_000, bytes_accessed=4 * 2**20, transcendentals=0
        ),
    )(place, *tokens, *columns)


def in_order(first, second, swap):
    return jnp.where(swap, second, first), jnp.where(swap, first, second)


def per_device(queries, long_keys, long_values, short_keys, short_values, w_out):
    rows = queries.shape[0]
    seq = lax.axis_index("seq")
    head = lax.axis_index("head")
    x, half, y = seq // (HS * YS), seq // YS % HS, seq % YS
    z, c = head // CS, head % CS

    first_up = {0: 5, 2: 7, 4: 8, 6: 10, 9: 12, 11: 14, 13: 1, 15: 3}
    second_up = {first_up[spot]: (spot + 8) % 16 for spot in first_up}
    stay = [spot for spot in range(16) if spot not in first_up]
    first_up.update({spot: spot ^ 1 for spot in stay})
    first_down = {spot: (spot - 4) % 16 for spot in stay}
    second_down = {first_down[spot]: (spot ^ 1) ^ 8 for spot in stay}

    def along(table):
        def target(x, h, y, z, c):
            to = table.get(h * ZS + z)
            return None if to is None else (x, to // ZS, y, to % ZS, c)

        return target

    upward, downward = moved(w_out, along(first_up)), moved(w_out, along(first_down))

    piece = jnp.stack([long_keys, long_values, short_keys, short_values])
    before = later(piece, 1)
    older = [later(piece[:2], steps) for steps in range(2, W1 // rows + 1)]
    mine = pack((long_keys, long_values, short_keys, short_values), before, older)
    lines = [[z * CS + core for z in range(ZS)] for core in range(CS)]
    mine, upward, downward = lax.optimization_barrier((mine, upward, downward))
    long_way, downward = moved(upward, along(second_up)), moved(downward, along(second_down))
    over_z = lax.all_to_all(mine, "head", 0, 0, axis_index_groups=lines, tiled=True)
    over_core = moved(over_z, lambda x, h, y, z, c: (x, h, y, z, 1 - c))

    near_by = half == z % 2
    pair = jnp.stack(
        [jnp.where(near_by, w_out, long_way), jnp.where(near_by, upward, downward)]
    )
    pair, over_core = lax.optimization_barrier((pair, over_core))
    from_x = [pair] + [
        moved(pair, lambda x, h, y, z, c, d=d: (x - d, h, y, z, c)) for d in (1, 2)
    ]

    attended = attention(jnp.stack([seq, c]), queries, over_z, over_core)
    attended, last = lax.optimization_barrier((attended, pair))
    last = moved(last, lambda x, h, y, z, c: (x - 3, h, y, z, c))

    beside = moved(attended, lambda x, h, y, z, c: (x, h, y, z ^ 1, c))
    beside, from_x = lax.optimization_barrier((beside, from_x))
    attended = jnp.stack([attended, beside])
    from_y = [attended] + [
        moved(attended, lambda x, h, y, z, c, d=d: (x, h, y - d, z, c)) for d in (1, 2, 3)
    ]
    sums = project(jnp.stack([x, y, z // 2, c]), from_y, from_x + [last])
    came = moved(sums[1], lambda x, h, y, z, c: (x, h, y, z, 1 - c))
    kept = (sums[0].astype(jnp.float32) + came.astype(jnp.float32)).astype(jnp.bfloat16)
    parts = [kept[0]] + [
        moved(kept[k], lambda x, h, y, z, c, k=k: (x, h, y, z ^ (2 * k), c)) for k in (3, 2, 1)
    ]
    summed = sum(part.astype(jnp.float32) for part in parts).astype(jnp.bfloat16)
    odd = y % 2 == 1
    sent = in_order(summed[0], summed[1], odd)
    landed = [
        moved(
            sent[j],
            lambda x, h, y, z, c, j=j: (x, h, 2 * c + (j ^ (y % 2)), z, y // 2),
        )
        for j in range(2)
    ]
    return jnp.concatenate(in_order(landed[0], landed[1], odd), axis=1)


def solution(mesh):
    return jax.shard_map(
        per_device,
        mesh=mesh,
        in_specs=(
            P("seq", "head"),
            P(("seq", "head"), None),
            P(("seq", "head"), None),
            P(("seq", "head"), None),
            P(("seq", "head"), None),
            P("head", "seq"),
        ),
        out_specs=P("seq", "head"),
        check_vma=False,
    )
```

```python
import functools
import math

import jax
import jax.numpy as jnp
from jax import lax
from jax.experimental import pallas as pl
from jax.experimental.pallas import tpu as pltpu
from jax.sharding import PartitionSpec as P

W1 = 512
W2 = 32
XS, HS, YS, ZS, CS = 4, 2, 4, 8, 2
BOTH = ("seq", "head")


def seq_of(x, half, y):
    return (x % XS) * HS * YS + (half % HS) * YS + y % YS


def moved(value, target):
    pairs = []
    for x in range(XS):
        for half in range(HS):
            for y in range(YS):
                for z in range(ZS):
                    for c in range(CS):
                        to = target(x, half, y, z, c)
                        if to is None:
                            continue
                        source = seq_of(x, half, y) * ZS * CS + z * CS + c
                        pairs.append((source, seq_of(*to[:3]) * ZS * CS + to[3] * CS + to[4]))
    return lax.ppermute(value, BOTH, pairs)


def later(value, steps):
    count = XS * HS * YS
    return lax.ppermute(value, "seq", [(s, s + steps) for s in range(count - steps)])


def attention_kernel(
    place, q_ref, mine_ref, other_ref, out_ref, k_ref, v_ref, sk_ref, sv_ref, q32, out32, *, tokens
):
    rows, wide = q_ref.shape
    width = k_ref.shape[1]
    heads = wide // width
    block_now, core = place[0], place[1]
    spots = W1 // rows + 1

    def whole(number):
        mine = mine_ref[:, number].astype(jnp.float32)
        other = other_ref[:, number].astype(jnp.float32)
        first, second = jnp.where(core == 1, other, mine), jnp.where(core == 1, mine, other)
        return jnp.concatenate([first[:, None], second[:, None]], axis=1).reshape(rows, width)

    for spot in reversed(range(spots)):
        there = block_now + spot >= spots - 1
        span = pl.ds(spot * rows, rows)
        k_ref[span, :] = whole(spot).astype(jnp.bfloat16)
        v_ref[span, :width] = whole(spots + spot).astype(jnp.bfloat16)
        v_ref[span, width:] = jnp.full((rows, width), jnp.where(there, 1.0, 0.0)).astype(jnp.bfloat16)
    for spot in range(1, spots):

        @pl.when(block_now == spots - 1 - spot)
        def _():
            key = whole(spot)[:1]
            filler = jnp.broadcast_to(key, (spot * rows, width))
            k_ref[: spot * rows, :] = filler.astype(jnp.bfloat16)

    short = whole(2 * spots + 2)
    sk_ref[W2:, :] = short
    edge = whole(2 * spots)[rows - W2 :]
    sk_ref[:W2, :] = jnp.where(block_now == 0, jnp.broadcast_to(short[:1], edge.shape), edge)
    sv_ref[W2:, :] = whole(2 * spots + 3)
    sv_ref[:W2, :] = whole(2 * spots + 1)[rows - W2 :]
    origin = block_now * rows

    span = sk_ref.shape[0] - rows
    factor = 2.5 / math.sqrt(width) * math.log2(math.e)
    q32[...] = q_ref[...].astype(jnp.float32)
    lanes = lax.broadcasted_iota(jnp.int32, (tokens, span, width), 2)
    token_of = lax.broadcasted_iota(jnp.int32, (tokens, span, width), 0)
    back = span - 1 - lax.broadcasted_iota(jnp.int32, (tokens, span, width), 1)

    def block(number, carry):
        start = pl.multiple_of(number * tokens, tokens)
        late = (lanes > start + token_of).reshape(tokens * span, width)
        counted = (origin + start + token_of >= back).astype(jnp.float32)
        keys = jnp.stack([sk_ref[pl.ds(start + 1 + i, span), :] for i in range(tokens)])
        values = jnp.stack([sv_ref[pl.ds(start + 1 + i, span), :] for i in range(tokens)])
        for head in range(heads):
            cols = slice(head * width, (head + 1) * width)
            chosen = q32[pl.ds(start, tokens), cols]
            mixed = (chosen[:, None, :] * keys).astype(jnp.bfloat16).reshape(tokens * span, width)
            scores = lax.dot_general(
                mixed, k_ref[...], (((1,), (1,)), ((), ())), preferred_element_type=jnp.float32
            )
            parts = [scores[:, i * width : (i + 1) * width] for i in range(5)]
            parts = [jnp.where(late, parts[0], parts[4])] + parts[1:4]
            top = jnp.maximum(jnp.maximum(parts[0], parts[1]), jnp.maximum(parts[2], parts[3]))
            top = jnp.max(top.reshape(tokens, span, width), axis=1)
            top = jnp.max(top, axis=1, keepdims=True)
            top = jnp.broadcast_to(top[:, :, None], (tokens, span, width))
            top = top.reshape(tokens * span, width)
            weights = [jnp.exp2((p - top) * factor) for p in parts]
            probs = [jnp.where(late, weights[0], 0.0)] + weights[1:]
            probs = probs + [jnp.where(late, 0.0, weights[0])]
            probs = jnp.concatenate([p.astype(jnp.bfloat16) for p in probs], axis=1)
            carried = jnp.dot(probs, v_ref[...], preferred_element_type=jnp.float32)
            above = jnp.sum(carried[:, :width].reshape(tokens, span, width) * values, axis=1)
            below = jnp.sum(carried[:, width:].reshape(tokens, span, width) * counted, axis=1)
            out32[pl.ds(start, tokens), cols] = above / below
        return carry

    lax.fori_loop(0, rows // tokens, block, 0)
    out_ref[...] = out32[...].astype(jnp.bfloat16)


def attention(place, q, mine, other):
    rows, wide = q.shape
    width = mine.shape[-1]
    spots = W1 // rows + 1
    return pl.pallas_call(
        functools.partial(attention_kernel, tokens=32),
        out_shape=jax.ShapeDtypeStruct((rows, wide), jnp.bfloat16),
        in_specs=[pl.BlockSpec(memory_space=pltpu.SMEM)]
        + [pl.BlockSpec(memory_space=pltpu.VMEM)] * 3,
        out_specs=pl.BlockSpec(memory_space=pltpu.VMEM),
        scratch_shapes=[
            pltpu.VMEM((spots * rows, width), jnp.bfloat16),
            pltpu.VMEM((spots * rows, 2 * width), jnp.bfloat16),
            pltpu.VMEM((W2 + rows, width), jnp.float32),
            pltpu.VMEM((W2 + rows, width), jnp.float32),
            pltpu.VMEM((rows, wide), jnp.float32),
            pltpu.VMEM((rows, wide), jnp.float32),
        ],
        compiler_params=pltpu.CompilerParams(vmem_limit_bytes=40 * 2**20),
        cost_estimate=pl.CostEstimate(
            flops=20_000_000_000, bytes_accessed=2**20, transcendentals=0
        ),
    )(place, q, mine, other)


def pack_kernel(count, *refs):
    own, before, older, out_ref = refs[:4], refs[4], refs[5:-1], refs[-1]
    for to in range(out_ref.shape[0]):
        for kind in range(2):
            line = [ref.at[kind] for ref in older[::-1]] + [before.at[kind], own[kind]]
            for spot, ref in enumerate(line):
                out_ref[to, kind * count + spot] = ref[...]
            out_ref[to, 2 * count + kind] = before[2 + kind]
            out_ref[to, 2 * count + 2 + kind] = own[2 + kind][...]


def pack(own, before, older):
    count = len(older) + 2
    return pl.pallas_call(
        functools.partial(pack_kernel, count),
        out_shape=jax.ShapeDtypeStruct((ZS, 2 * count + 4) + own[0].shape, own[0].dtype),
        in_specs=[pl.BlockSpec(memory_space=pltpu.VMEM)] * (5 + len(older)),
        out_specs=pl.BlockSpec(memory_space=pltpu.VMEM),
    )(*own, before, *older)


def project_kernel(place, *refs):
    tokens, columns, out_ref = refs[:YS], refs[YS : YS + XS], refs[-1]
    x, y, far, c = place[0], place[1], place[2], place[3]
    for d in range(XS):
        to = lax.rem(x + d, XS) ^ far
        for e in range(YS):
            slot = lax.rem(y + e + YS - 2 * c, YS)
            total = jnp.dot(tokens[e][0], columns[d][0], preferred_element_type=jnp.float32)
            total += jnp.dot(tokens[e][1], columns[d][1], preferred_element_type=jnp.float32)
            out_ref[slot // 2, to, slot % 2] = total.astype(jnp.bfloat16)


def project(place, tokens, columns):
    rows, wide = tokens[0].shape[1], columns[0].shape[2]
    return pl.pallas_call(
        project_kernel,
        out_shape=jax.ShapeDtypeStruct((2, XS, YS // 2, rows, wide), jnp.bfloat16),
        in_specs=[pl.BlockSpec(memory_space=pltpu.SMEM)]
        + [pl.BlockSpec(memory_space=pltpu.VMEM)] * (XS + YS),
        out_specs=pl.BlockSpec(memory_space=pltpu.VMEM),
        compiler_params=pltpu.CompilerParams(vmem_limit_bytes=40 * 2**20),
        cost_estimate=pl.CostEstimate(
            flops=1_100_000_000, bytes_accessed=4 * 2**20, transcendentals=0
        ),
    )(place, *tokens, *columns)


def in_order(first, second, swap):
    return jnp.where(swap, second, first), jnp.where(swap, first, second)


def per_device(queries, long_keys, long_values, short_keys, short_values, w_out):
    rows = queries.shape[0]
    seq = lax.axis_index("seq")
    head = lax.axis_index("head")
    x, half, y = seq // (HS * YS), seq // YS % HS, seq % YS
    z, c = head // CS, head % CS

    first_up = {0: 5, 2: 7, 4: 8, 6: 10, 9: 12, 11: 14, 13: 1, 15: 3}
    second_up = {first_up[spot]: (spot + 8) % 16 for spot in first_up}
    stay = [spot for spot in range(16) if spot not in first_up]
    first_up.update({spot: spot ^ 1 for spot in stay})
    first_down = {spot: (spot - (5 if spot < 8 else 4)) % 16 for spot in stay}
    second_down = {first_down[spot]: (spot ^ 1) ^ 8 for spot in stay}

    def along(table):
        def target(x, h, y, z, c):
            to = table.get(h * ZS + z)
            return None if to is None else (x, to // ZS, y, to % ZS, c)

        return target

    upward, downward = moved(w_out, along(first_up)), moved(w_out, along(first_down))

    piece = jnp.stack([long_keys, long_values, short_keys, short_values])
    before = later(piece, 1)
    older = [later(piece[:2], steps) for steps in range(2, W1 // rows + 1)]
    mine = pack((long_keys, long_values, short_keys, short_values), before, older)
    lines = [[z * CS + core for z in range(ZS)] for core in range(CS)]
    mine, upward, downward = lax.optimization_barrier((mine, upward, downward))
    long_way, downward = moved(upward, along(second_up)), moved(downward, along(second_down))
    over_z = lax.all_to_all(mine, "head", 0, 0, axis_index_groups=lines, tiled=True)
    over_core = moved(over_z, lambda x, h, y, z, c: (x, h, y, z, 1 - c))

    near_by = half == z % 2
    pair = jnp.stack(
        [jnp.where(near_by, w_out, long_way), jnp.where(near_by, upward, downward)]
    )
    pair, over_core = lax.optimization_barrier((pair, over_core))
    from_x = [pair] + [
        moved(pair, lambda x, h, y, z, c, d=d: (x - d, h, y, z, c)) for d in (1, 2)
    ]

    attended = attention(jnp.stack([seq, c]), queries, over_z, over_core)
    attended, last = lax.optimization_barrier((attended, pair))
    last = moved(last, lambda x, h, y, z, c: (x - 3, h, y, z, c))

    beside = moved(attended, lambda x, h, y, z, c: (x, h, y, z ^ 1, c))
    beside, from_x = lax.optimization_barrier((beside, from_x))
    attended = jnp.stack([attended, beside])
    from_y = [attended] + [
        moved(attended, lambda x, h, y, z, c, d=d: (x, h, y - d, z, c)) for d in (1, 2, 3)
    ]
    sums = project(jnp.stack([x, y, z // 2, c]), from_y, from_x + [last])
    came = moved(sums[1], lambda x, h, y, z, c: (x, h, y, z, 1 - c))
    kept = (sums[0].astype(jnp.float32) + came.astype(jnp.float32)).astype(jnp.bfloat16)
    parts = [kept[0]] + [
        moved(kept[k], lambda x, h, y, z, c, k=k: (x, h, y, z ^ (2 * k), c)) for k in (3, 2, 1)
    ]
    summed = sum(part.astype(jnp.float32) for part in parts).astype(jnp.bfloat16)
    odd = y % 2 == 1
    sent = in_order(summed[0], summed[1], odd)
    landed = [
        moved(
            sent[j],
            lambda x, h, y, z, c, j=j: (x, h, 2 * c + (j ^ (y % 2)), z, y // 2),
        )
        for j in range(2)
    ]
    return jnp.concatenate(in_order(landed[0], landed[1], odd), axis=1)


def solution(mesh):
    return jax.shard_map(
        per_device,
        mesh=mesh,
        in_specs=(
            P("seq", "head"),
            P(("seq", "head"), None),
            P(("seq", "head"), None),
            P(("seq", "head"), None),
            P(("seq", "head"), None),
            P("head", "seq"),
        ),
        out_specs=P("seq", "head"),
        check_vma=False,
    )
```

```python
import functools
import math

import jax
import jax.numpy as jnp
from jax import lax
from jax.experimental import pallas as pl
from jax.experimental.pallas import tpu as pltpu
from jax.sharding import PartitionSpec as P

W1 = 512
W2 = 32
XS, HS, YS, ZS, CS = 4, 2, 4, 8, 2
BOTH = ("seq", "head")


def seq_of(x, half, y):
    return (x % XS) * HS * YS + (half % HS) * YS + y % YS


def moved(value, target):
    pairs = []
    for x in range(XS):
        for half in range(HS):
            for y in range(YS):
                for z in range(ZS):
                    for c in range(CS):
                        to = target(x, half, y, z, c)
                        if to is None:
                            continue
                        source = seq_of(x, half, y) * ZS * CS + z * CS + c
                        pairs.append((source, seq_of(*to[:3]) * ZS * CS + to[3] * CS + to[4]))
    return lax.ppermute(value, BOTH, pairs)


def later(value, steps):
    count = XS * HS * YS
    return lax.ppermute(value, "seq", [(s, s + steps) for s in range(count - steps)])


def attention_kernel(
    place, q_ref, mine_ref, other_ref, out_ref, k_ref, v_ref, sk_ref, sv_ref, q32, out32, *, tokens
):
    rows, wide = q_ref.shape
    width = k_ref.shape[1]
    heads = wide // width
    block_now, core = place[0], place[1]
    spots = W1 // rows + 1

    def whole(number):
        mine = mine_ref[:, number].astype(jnp.float32)
        other = other_ref[:, number].astype(jnp.float32)
        first, second = jnp.where(core == 1, other, mine), jnp.where(core == 1, mine, other)
        return jnp.concatenate([first[:, None], second[:, None]], axis=1).reshape(rows, width)

    for spot in reversed(range(spots)):
        there = block_now + spot >= spots - 1
        span = pl.ds(spot * rows, rows)
        k_ref[span, :] = whole(spot).astype(jnp.bfloat16)
        v_ref[span, :width] = whole(spots + spot).astype(jnp.bfloat16)
        v_ref[span, width:] = jnp.full((rows, width), jnp.where(there, 1.0, 0.0)).astype(jnp.bfloat16)
    for spot in range(1, spots):

        @pl.when(block_now == spots - 1 - spot)
        def _():
            key = whole(spot)[:1]
            filler = jnp.broadcast_to(key, (spot * rows, width))
            k_ref[: spot * rows, :] = filler.astype(jnp.bfloat16)

    short = whole(2 * spots + 2)
    sk_ref[W2:, :] = short
    edge = whole(2 * spots)[rows - W2 :]
    sk_ref[:W2, :] = jnp.where(block_now == 0, jnp.broadcast_to(short[:1], edge.shape), edge)
    sv_ref[W2:, :] = whole(2 * spots + 3)
    sv_ref[:W2, :] = whole(2 * spots + 1)[rows - W2 :]
    origin = block_now * rows

    span = sk_ref.shape[0] - rows
    factor = 2.5 / math.sqrt(width) * math.log2(math.e)
    q32[...] = q_ref[...].astype(jnp.float32)
    lanes = lax.broadcasted_iota(jnp.int32, (tokens, span, width), 2)
    token_of = lax.broadcasted_iota(jnp.int32, (tokens, span, width), 0)
    back = span - 1 - lax.broadcasted_iota(jnp.int32, (tokens, span, width), 1)

    def block(number, carry):
        start = pl.multiple_of(number * tokens, tokens)
        late = (lanes > start + token_of).reshape(tokens * span, width)
        counted = (origin + start + token_of >= back).astype(jnp.float32)
        keys = jnp.stack([sk_ref[pl.ds(start + 1 + i, span), :] for i in range(tokens)])
        values = jnp.stack([sv_ref[pl.ds(start + 1 + i, span), :] for i in range(tokens)])
        for head in range(heads):
            cols = slice(head * width, (head + 1) * width)
            chosen = q32[pl.ds(start, tokens), cols]
            mixed = (chosen[:, None, :] * keys).astype(jnp.bfloat16).reshape(tokens * span, width)
            scores = lax.dot_general(
                mixed, k_ref[...], (((1,), (1,)), ((), ())), preferred_element_type=jnp.float32
            )
            parts = [scores[:, i * width : (i + 1) * width] for i in range(5)]
            parts = [jnp.where(late, parts[0], parts[4])] + parts[1:4]
            top = jnp.maximum(jnp.maximum(parts[0], parts[1]), jnp.maximum(parts[2], parts[3]))
            top = jnp.max(top.reshape(tokens, span, width), axis=1)
            top = jnp.max(top, axis=1, keepdims=True)
            top = jnp.broadcast_to(top[:, :, None], (tokens, span, width))
            top = top.reshape(tokens * span, width)
            weights = [jnp.exp2((p - top) * factor) for p in parts]
            probs = [jnp.where(late, weights[0], 0.0)] + weights[1:]
            probs = probs + [jnp.where(late, 0.0, weights[0])]
            probs = jnp.concatenate([p.astype(jnp.bfloat16) for p in probs], axis=1)
            carried = jnp.dot(probs, v_ref[...], preferred_element_type=jnp.float32)
            above = jnp.sum(carried[:, :width].reshape(tokens, span, width) * values, axis=1)
            below = jnp.sum(carried[:, width:].reshape(tokens, span, width) * counted, axis=1)
            out32[pl.ds(start, tokens), cols] = above / below
        return carry

    lax.fori_loop(0, rows // tokens, block, 0)
    out_ref[...] = out32[...].astype(jnp.bfloat16)


def attention(place, q, mine, other):
    rows, wide = q.shape
    width = mine.shape[-1]
    spots = W1 // rows + 1
    return pl.pallas_call(
        functools.partial(attention_kernel, tokens=32),
        out_shape=jax.ShapeDtypeStruct((rows, wide), jnp.bfloat16),
        in_specs=[pl.BlockSpec(memory_space=pltpu.SMEM)]
        + [pl.BlockSpec(memory_space=pltpu.VMEM)] * 3,
        out_specs=pl.BlockSpec(memory_space=pltpu.VMEM),
        scratch_shapes=[
            pltpu.VMEM((spots * rows, width), jnp.bfloat16),
            pltpu.VMEM((spots * rows, 2 * width), jnp.bfloat16),
            pltpu.VMEM((W2 + rows, width), jnp.float32),
            pltpu.VMEM((W2 + rows, width), jnp.float32),
            pltpu.VMEM((rows, wide), jnp.float32),
            pltpu.VMEM((rows, wide), jnp.float32),
        ],
        compiler_params=pltpu.CompilerParams(vmem_limit_bytes=40 * 2**20),
        cost_estimate=pl.CostEstimate(
            flops=20_000_000_000, bytes_accessed=2**20, transcendentals=0
        ),
    )(place, q, mine, other)


def pack_kernel(count, *refs):
    own, before, older, out_ref = refs[:4], refs[4], refs[5:-1], refs[-1]
    for to in range(out_ref.shape[0]):
        for kind in range(2):
            line = [ref.at[kind] for ref in older[::-1]] + [before.at[kind], own[kind]]
            for spot, ref in enumerate(line):
                out_ref[to, kind * count + spot] = ref[...]
            out_ref[to, 2 * count + kind] = before[2 + kind]
            out_ref[to, 2 * count + 2 + kind] = own[2 + kind][...]


def pack(own, before, older):
    count = len(older) + 2
    return pl.pallas_call(
        functools.partial(pack_kernel, count),
        out_shape=jax.ShapeDtypeStruct((ZS, 2 * count + 4) + own[0].shape, own[0].dtype),
        in_specs=[pl.BlockSpec(memory_space=pltpu.VMEM)] * (5 + len(older)),
        out_specs=pl.BlockSpec(memory_space=pltpu.VMEM),
    )(*own, before, *older)


def project_kernel(place, *refs):
    tokens, columns, out_ref = refs[:YS], refs[YS : YS + XS], refs[-1]
    x, y, far, c = place[0], place[1], place[2], place[3]
    for d in range(XS):
        to = lax.rem(x + d, XS) ^ far
        for e in range(YS):
            slot = lax.rem(y + e + YS - 2 * c, YS)
            total = jnp.dot(tokens[e][0], columns[d][0], preferred_element_type=jnp.float32)
            total += jnp.dot(tokens[e][1], columns[d][1], preferred_element_type=jnp.float32)
            out_ref[slot // 2, to, slot % 2] = total.astype(jnp.bfloat16)


def project(place, tokens, columns):
    rows, wide = tokens[0].shape[1], columns[0].shape[2]
    return pl.pallas_call(
        project_kernel,
        out_shape=jax.ShapeDtypeStruct((2, XS, YS // 2, rows, wide), jnp.bfloat16),
        in_specs=[pl.BlockSpec(memory_space=pltpu.SMEM)]
        + [pl.BlockSpec(memory_space=pltpu.VMEM)] * (XS + YS),
        out_specs=pl.BlockSpec(memory_space=pltpu.VMEM),
        compiler_params=pltpu.CompilerParams(vmem_limit_bytes=40 * 2**20),
        cost_estimate=pl.CostEstimate(
            flops=1_100_000_000, bytes_accessed=4 * 2**20, transcendentals=0
        ),
    )(place, *tokens, *columns)


def in_order(first, second, swap):
    return jnp.where(swap, second, first), jnp.where(swap, first, second)


def per_device(queries, long_keys, long_values, short_keys, short_values, w_out):
    rows = queries.shape[0]
    seq = lax.axis_index("seq")
    head = lax.axis_index("head")
    x, half, y = seq // (HS * YS), seq // YS % HS, seq % YS
    z, c = head // CS, head % CS

    first_up = {0: 5, 2: 7, 4: 8, 6: 10, 9: 12, 11: 14, 13: 1, 15: 3}
    second_up = {first_up[spot]: (spot + 8) % 16 for spot in first_up}
    stay = [spot for spot in range(16) if spot not in first_up]
    first_up.update({spot: spot ^ 1 for spot in stay})
    first_down = {spot: (spot - (5 if spot < 4 else 4)) % 16 for spot in stay}
    second_down = {first_down[spot]: (spot ^ 1) ^ 8 for spot in stay}

    def along(table):
        def target(x, h, y, z, c):
            to = table.get(h * ZS + z)
            return None if to is None else (x, to // ZS, y, to % ZS, c)

        return target

    upward, downward = moved(w_out, along(first_up)), moved(w_out, along(first_down))

    piece = jnp.stack([long_keys, long_values, short_keys, short_values])
    before = later(piece, 1)
    older = [later(piece[:2], steps) for steps in range(2, W1 // rows + 1)]
    mine = pack((long_keys, long_values, short_keys, short_values), before, older)
    lines = [[z * CS + core for z in range(ZS)] for core in range(CS)]
    mine, upward, downward = lax.optimization_barrier((mine, upward, downward))
    long_way, downward = moved(upward, along(second_up)), moved(downward, along(second_down))
    over_z = lax.all_to_all(mine, "head", 0, 0, axis_index_groups=lines, tiled=True)
    over_core = moved(over_z, lambda x, h, y, z, c: (x, h, y, z, 1 - c))

    near_by = half == z % 2
    pair = jnp.stack(
        [jnp.where(near_by, w_out, long_way), jnp.where(near_by, upward, downward)]
    )
    pair, over_core = lax.optimization_barrier((pair, over_core))
    from_x = [pair] + [
        moved(pair, lambda x, h, y, z, c, d=d: (x - d, h, y, z, c)) for d in (1, 2)
    ]

    attended = attention(jnp.stack([seq, c]), queries, over_z, over_core)
    attended, last = lax.optimization_barrier((attended, pair))
    last = moved(last, lambda x, h, y, z, c: (x - 3, h, y, z, c))

    beside = moved(attended, lambda x, h, y, z, c: (x, h, y, z ^ 1, c))
    beside, from_x = lax.optimization_barrier((beside, from_x))
    attended = jnp.stack([attended, beside])
    from_y = [attended] + [
        moved(attended, lambda x, h, y, z, c, d=d: (x, h, y - d, z, c)) for d in (1, 2, 3)
    ]
    sums = project(jnp.stack([x, y, z // 2, c]), from_y, from_x + [last])
    came = moved(sums[1], lambda x, h, y, z, c: (x, h, y, z, 1 - c))
    kept = (sums[0].astype(jnp.float32) + came.astype(jnp.float32)).astype(jnp.bfloat16)
    parts = [kept[0]] + [
        moved(kept[k], lambda x, h, y, z, c, k=k: (x, h, y, z ^ (2 * k), c)) for k in (3, 2, 1)
    ]
    summed = sum(part.astype(jnp.float32) for part in parts).astype(jnp.bfloat16)
    odd = y % 2 == 1
    sent = in_order(summed[0], summed[1], odd)
    landed = [
        moved(
            sent[j],
            lambda x, h, y, z, c, j=j: (x, h, 2 * c + (j ^ (y % 2)), z, y // 2),
        )
        for j in range(2)
    ]
    return jnp.concatenate(in_order(landed[0], landed[1], odd), axis=1)


def solution(mesh):
    return jax.shard_map(
        per_device,
        mesh=mesh,
        in_specs=(
            P("seq", "head"),
            P(("seq", "head"), None),
            P(("seq", "head"), None),
            P(("seq", "head"), None),
            P(("seq", "head"), None),
            P("head", "seq"),
        ),
        out_specs=P("seq", "head"),
        check_vma=False,
    )
```
